128 devices in a mesh: member: 8 (over y, z_hi), space: 16 (over x, z_lo, core).
Axes of the slice: x: 4, y: 4, z: 4 (z_hi: 2, z_lo: 2; z = z_hi * 2 + z_lo), core: 2. Of those that a mesh axis runs over, the one named last changes fastest.
Arguments:
- latent: bfloat16 [16, 2048, 1024], P('member', 'space'), may hold values from -17 to 17
- predictions: float32 [16, 100, 2048], P('member', None, 'space'), may hold values from -6 to 6
- target: float32 [100, 2048], P(None, 'space'), may hold values from -6 to 6
- area_weight: float32 [2048], P('space'), may hold values from 0.1 to 1
- slab_count: int32 [16], P('space'), may hold values from 64 to 128, as said below
- w_qkv: bfloat16 [1024, 3072], replicated, may hold values from -4 to 4
- w_o: bfloat16 [1024, 1024], replicated, may hold values from -0.1875 to 0.1875
- w_out: bfloat16 [1024, 100], replicated, may hold values from -0.1875 to 0.1875
Outputs:
- grad_latent: bfloat16 [16, 2048, 1024], P('member', 'space')
- grad_qkv: float32 [1024, 3072], P(('member', 'space'))
- grad_o: float32 [1024, 1024], P(('member', 'space'))
- grad_out: float32 [1024, 100], P(('member', 'space'))
The draws below stay inside these ranges and needn't reach their ends.
Inputs may be any that keep to these rules, and one draw needn't show every extreme that they name: `slab_count`: at least one slab has all 128 slots live.
All inputs are finite; a program needn't handle non-finite values.
Results may differ from the reference program's by a relative error of at most 0.03.
The reference program's roundings to bfloat16 on the way count: a program that leaves them out, or rounds other values in their place, can miss the bound.
Values may be sent and summed in bfloat16 or wider, within the bound.
A program may use at most 128 MiB of HBM per device.

```python
import math
import jax
import jax.numpy as jnp
from jax import lax

D = 1024
HEAD_DIM = 64
CHANNELS = 100
BLOCK = 128
MEM_DEV = 2
P_DEV = 128
MEMBERS = 16
POINTS = 2048
N_MEMBER = 8
N_SPACE = 16


def draw_slab_count(key, part):
    key = jax.random.fold_in(key, 7)
    first_key, second_key = jax.random.split(key)
    counts = jax.random.randint(first_key, (N_SPACE,), P_DEV // 2, P_DEV + 1)
    fullest = jax.random.randint(second_key, (), 0, N_SPACE)
    return jnp.where(jnp.arange(N_SPACE) == fullest, P_DEV, counts).astype(jnp.int32)


def draw_latent(key, part):
    key = jax.random.fold_in(key, 11)
    value_key, pair_key = jax.random.split(key, 2)
    shape = (MEMBERS, POINTS, D)
    values = jax.random.truncated_normal(value_key, -4.0, 4.0, shape, jnp.float32)
    devices_all = N_MEMBER * N_SPACE
    pairing = jax.random.permutation(pair_key, devices_all)
    owner = (jnp.arange(MEMBERS) // MEM_DEV)[:, None] * N_SPACE + (jnp.arange(POINTS) // P_DEV)[None, :]
    feature_block = jnp.arange(D) // (D // devices_all)
    boosted = pairing[owner][:, :, None] == feature_block[None, None, :]
    values = values * jnp.where(boosted, 4.0, 1.0)
    return values.astype(jnp.bfloat16)


def draw_w_qkv(key, part):
    key = jax.random.fold_in(key, 13)
    weight_key = jax.random.fold_in(key, 0)
    values = jax.random.truncated_normal(weight_key, -4.0, 4.0, (D, 3 * D), jnp.float32) * D ** (-0.5)
    return values.astype(jnp.bfloat16)


def shard_levels(own_key, dims, pieces, least, high):
    def one(position, parts):
        draws = jax.random.uniform(jax.random.fold_in(jax.random.fold_in(own_key, 6), position), (parts,), jnp.float32, least / len(pieces), high / len(pieces))
        return jnp.repeat(jnp.exp(draws), dims[position] // parts).reshape((-1,) + (1,) * (len(dims) - position - 1))

    loudness = one(*pieces[0])
    for cut in pieces[1:]:
        loudness = loudness * one(*cut)
    return loudness


def gaussian(own_key, dims, spread, limit, shards=(), held_as=jnp.bfloat16):
    result = spread * jax.random.normal(own_key, dims, jnp.float32)
    if shards:
        result = result * shard_levels(own_key, dims, shards, -0.22, 0.18)
    return jnp.clip(result, -limit, limit).astype(held_as)


def setup_inputs(seed: int = 0) -> dict:
    splits = jax.random.split(jax.random.key(seed), 9)
    return {
        "latent": draw_latent(jax.random.fold_in(splits[8], 71), 0),
        "predictions": gaussian(splits[1], (MEMBERS, CHANNELS, POINTS), 1.0, 6.0, ((0, 8), (2, 16)), jnp.float32),
        "target": gaussian(splits[2], (CHANNELS, POINTS), 1.0, 6.0, ((1, 16),), jnp.float32),
        "area_weight": jnp.clip(jnp.exp(math.log(1.0) - 2.3025851 * jax.random.uniform(splits[3], (POINTS,), jnp.float32) ** shard_levels(splits[3], (POINTS,), ((0, 16),), -0.2, 0.2)), 0.1, 1.0),
        "slab_count": draw_slab_count(jax.random.fold_in(splits[8], 71), 0),
        "w_qkv": draw_w_qkv(jax.random.fold_in(splits[8], 71), 0),
        "w_o": gaussian(splits[6], (D, D), D ** -0.5, 0.1875),
        "w_out": gaussian(splits[7], (D, CHANNELS), D ** -0.5, 0.1875),
    }


def reference(latent, predictions, target, area_weight, slab_count, w_qkv, w_o, w_out):
    members = latent.shape[0]
    points = latent.shape[1]
    width = latent.shape[2]
    place = jnp.arange(points)
    live = place % P_DEV < slab_count[place // P_DEV]
    pweight = jnp.where(live, area_weight, jnp.zeros_like(area_weight))

    def member_grad(own):
        first = jnp.sign(own - target)
        pair = lax.optimization_barrier(jnp.sum(jnp.sign(own[None] - predictions), axis=0))
        return pweight[None, :] * (first - pair / (members - 1))
    crps = lax.map(member_grad, predictions)
    nblk = points // BLOCK
    heads = width // HEAD_DIM
    scale = HEAD_DIM ** (-0.5)
    ext = jnp.arange(nblk)[:, None] + (jnp.arange(3 * BLOCK) // BLOCK)[None, :]
    valid = (ext >= 1) & (ext <= nblk)

    def step(carry, item):
        sum_qkv, sum_o, sum_out = carry
        xrow, grad = item
        xf = xrow.astype(jnp.float32)
        mean = lax.optimization_barrier(jnp.mean(xf, axis=-1, keepdims=True))
        cent = xf - mean
        var = lax.optimization_barrier(jnp.mean(cent * cent, axis=-1, keepdims=True))
        rstd = lax.rsqrt(var + 1e-05)
        norm = cent * rstd
        xn = norm.astype(jnp.bfloat16)
        qkv = jnp.dot(xn, w_qkv, preferred_element_type=jnp.float32).astype(jnp.bfloat16)
        query = qkv[:, :width]
        keyval = qkv[:, width:]
        zero = jnp.zeros((BLOCK, 2 * width), jnp.bfloat16)
        blocks = jnp.concatenate([zero, keyval, zero], axis=0).reshape(nblk + 2, BLOCK, 2 * width)
        window = jnp.concatenate([blocks[:-2], blocks[1:-1], blocks[2:]], axis=1)
        qh = query.reshape(nblk, BLOCK, heads, HEAD_DIM).astype(jnp.float32)
        kh = window[..., :width].reshape(nblk, 3 * BLOCK, heads, HEAD_DIM).astype(jnp.float32)
        vh = window[..., width:].reshape(nblk, 3 * BLOCK, heads, HEAD_DIM).astype(jnp.float32)
        scores = jnp.einsum('nqhd,nkhd->nhqk', qh, kh) * scale
        scores = jnp.where(valid[:, None, None, :], scores, -1e+30)
        prob = jax.nn.softmax(scores, axis=-1)
        prob_b = prob.astype(jnp.bfloat16)
        attended = jnp.einsum('nhqk,nkhd->nqhd', prob_b.astype(jnp.float32), vh)
        attended = attended.reshape(points, width).astype(jnp.bfloat16)
        after = (xf + jnp.dot(attended, w_o, preferred_element_type=jnp.float32)).astype(jnp.bfloat16)
        grad_b = grad.astype(jnp.bfloat16)
        dafter = jnp.dot(grad_b.T, w_out.T, preferred_element_type=jnp.float32)
        dafter_b = dafter.astype(jnp.bfloat16)
        term_out = jnp.dot(after.T, grad_b.T, preferred_element_type=jnp.float32)
        term_o = jnp.dot(attended.T, dafter_b, preferred_element_type=jnp.float32)
        dattend = jnp.dot(dafter_b, w_o.T, preferred_element_type=jnp.float32).astype(jnp.bfloat16)
        dah = dattend.reshape(nblk, BLOCK, heads, HEAD_DIM).astype(jnp.float32)
        dprob = jnp.einsum('nqhd,nkhd->nhqk', dah, vh)
        dval = jnp.einsum('nhqk,nqhd->nkhd', prob_b.astype(jnp.float32), dah)
        delta = lax.optimization_barrier(jnp.sum(dprob * prob, axis=-1, keepdims=True))
        dscore = (prob * (dprob - delta) * scale).astype(jnp.bfloat16).astype(jnp.float32)
        dquery = jnp.einsum('nhqk,nkhd->nqhd', dscore, kh).reshape(points, width)
        dkey = jnp.einsum('nhqk,nqhd->nkhd', dscore, qh)
        dwin = jnp.concatenate([dkey.reshape(nblk, 3 * BLOCK, width), dval.reshape(nblk, 3 * BLOCK, width)], axis=-1)
        dwin = dwin.reshape(nblk, 3, BLOCK, 2 * width)
        dwide = jnp.pad(dwin[:, 0], ((0, 2), (0, 0), (0, 0)))
        dwide = dwide + jnp.pad(dwin[:, 1], ((1, 1), (0, 0), (0, 0)))
        dwide = dwide + jnp.pad(dwin[:, 2], ((2, 0), (0, 0), (0, 0)))
        dkv = dwide[1:-1].reshape(points, 2 * width)
        dqkv = jnp.concatenate([dquery, dkv], axis=-1).astype(jnp.bfloat16)
        term_qkv = jnp.dot(xn.T, dqkv, preferred_element_type=jnp.float32)
        dnorm = jnp.dot(dqkv, w_qkv.T, preferred_element_type=jnp.float32)
        dlayer = rstd * (dnorm - lax.optimization_barrier(jnp.mean(dnorm, axis=-1, keepdims=True)) - norm * lax.optimization_barrier(jnp.mean(dnorm * norm, axis=-1, keepdims=True)))
        grad_row = (dafter + dlayer).astype(jnp.bfloat16)
        return ((sum_qkv + term_qkv, sum_o + term_o, sum_out + term_out), grad_row)
    start = (jnp.zeros((width, 3 * width), jnp.float32), jnp.zeros((width, width), jnp.float32), jnp.zeros((width, w_out.shape[1]), jnp.float32))
    sums, grad_latent = lax.scan(step, start, (latent, crps))
    return (grad_latent, sums[0], sums[1], sums[2])
```

```python
import functools

import jax
import jax.numpy as jnp
from jax import lax
from jax.experimental import pallas as pl
from jax.experimental.pallas import tpu as pltpu
from jax.sharding import PartitionSpec as P

HEAD_DIM = 64
BLOCK = 128
RING = 4
F32 = jnp.float32
BF16 = jnp.bfloat16

ORDERS = (("x", "y", "z"), ("y", "z", "x"), ("z", "x", "y"))
WIDTHS = (640, 768, 768)


class Place:
    def __init__(self):
        self.member = lax.axis_index("member")
        self.space = lax.axis_index("space")
        self.core = self.space % 2
        z_lo = (self.space // 2) % 2
        z_hi = self.member % 2
        self.at = {"x": self.space // 4, "y": self.member // 2, "z": z_hi * 2 + z_lo}

    def partner(self, axis, index):
        if axis == "x":
            return (self.member, index * 4 + self.space % 4)
        if axis == "y":
            return (index * 2 + self.member % 2, self.space)
        member = (self.member // 2) * 2 + index // 2
        return (member, (self.space // 4) * 4 + (index % 2) * 2 + self.core)

    def pair(self):
        return (self.member, self.space + 1 - 2 * self.core)

    def ahead(self, axis, offset):
        return (self.at[axis] + offset) % RING


def chunk_order(order):
    where = []
    for y in range(4):
        for z_hi in range(2):
            for x in range(4):
                for z_lo in range(2):
                    digit = {"x": x, "y": y, "z": z_hi * 2 + z_lo}
                    a, b, c = (digit[name] for name in order)
                    where.append(a * 16 + b * 4 + c)
    return where


def remote(src, dst, send, recv, device):
    return pltpu.make_async_remote_copy(
        src_ref=src,
        dst_ref=dst,
        send_sem=send,
        recv_sem=recv,
        device_id=device,
        device_id_type=pl.DeviceIdType.MESH,
    )


def dot(a, b):
    return jnp.dot(a, b, preferred_element_type=F32)


def reduce_kernel(
    xn, dqkv, att, daf, aft, crps, g_qkv, g_o, g_out,
    xn_o, att_o, d_q, d_k, d_v, d_o, xt_a, xt_b, xt_c, at_b, at_c, ft_a,
    send1_a, send1_b, send1_c, recv1_a, recv1_b, recv1_c, acc1_a, acc1_b, acc1_c,
    send2_a, send2_b, send2_c, recv2_a, recv2_b, recv2_c, acc2_a, acc2_b, acc2_c,
    recv3_a, recv3_b, recv3_c, fin_a, fin_b, fin_c, oth_a, oth_b, oth_c,
    pair_send, pair_recv, ring_send, ring_recv, last_send, last_recv,
):
    place = Place()
    core = place.core
    rows = xn.shape[0]
    half = 512

    barrier = pltpu.get_barrier_semaphore()
    pl.semaphore_signal(barrier, inc=1, device_id=place.pair(), device_id_type=pl.DeviceIdType.MESH)
    for axis in ("x", "y", "z"):
        for offset in (1, 2, 3):
            pl.semaphore_signal(
                barrier, inc=1, device_id=place.partner(axis, place.ahead(axis, offset)),
                device_id_type=pl.DeviceIdType.MESH,
            )
    pl.semaphore_wait(barrier, 10)

    theirs = pl.multiple_of((1 - core) * half, half)
    moves = [
        (xn, xn_o),
        (dqkv.at[:, pl.ds(theirs, half)], d_q.at[pl.ds(rows, rows)]),
        (dqkv.at[:, pl.ds(1024 + theirs, half)], d_k.at[pl.ds(rows, rows)]),
        (dqkv.at[:, pl.ds(2048 + theirs, half)], d_v.at[pl.ds(rows, rows)]),
        (att, att_o),
        (daf.at[:, pl.ds(theirs, half)], d_o.at[pl.ds(rows, rows)]),
    ]
    pair = [
        remote(src, dst, pair_send.at[i], pair_recv.at[i], place.pair())
        for i, (src, dst) in enumerate(moves)
    ]
    for copy in pair:
        copy.start()

    def mine(ref, start):
        return jnp.where(core == 0, ref[:, start : start + half], ref[:, start + half : start + 2 * half])

    d_q[:rows] = mine(dqkv, 0)
    d_k[:rows] = mine(dqkv, 1024)
    d_v[:rows] = mine(dqkv, 2048)
    d_o[:rows] = mine(daf, 0)

    def lay(value, targets, column):
        turned = value.T
        for ref, order in targets:
            for chunk, spot in enumerate(chunk_order(order)):
                ref[spot * 16 : spot * 16 + 16, column : column + rows] = turned[chunk * 16 : chunk * 16 + 16]

    xts = [(xt_a, ORDERS[0]), (xt_b, ORDERS[1]), (xt_c, ORDERS[2])]
    ats = [(at_b, ORDERS[1]), (at_c, ORDERS[2])]
    lay(xn[...], xts, 0)
    lay(att[...], ats, 0)
    lay(aft[...], [(ft_a, ORDERS[0])], 0)
    pair[0].wait_recv()
    lay(xn_o[...], xts, rows)
    pair[4].wait_recv()
    lay(att_o[...], ats, rows)
    for i in (1, 2, 3, 5):
        pair[i].wait_recv()

    def part(p, dest):
        rows_of = pl.ds(pl.multiple_of(dest * 256, 256), 256)
        if p == 0:
            return (dot(xt_a[rows_of], d_q[...]), dot(ft_a[rows_of], crps[...]))
        if p == 1:
            return (dot(xt_b[rows_of], d_k[...]), dot(at_b[rows_of], d_o[:, :256]))
        return (dot(xt_c[rows_of], d_v[...]), dot(at_c[rows_of], d_o[:, 256:]))

    send1, recv1, acc1 = (send1_a, send1_b, send1_c), (recv1_a, recv1_b, recv1_c), (acc1_a, acc1_b, acc1_c)
    send2, recv2, acc2 = (send2_a, send2_b, send2_c), (recv2_a, recv2_b, recv2_c), (acc2_a, acc2_b, acc2_c)
    recv3, fin, oth = (recv3_a, recv3_b, recv3_c), (fin_a, fin_b, fin_c), (oth_a, oth_b, oth_c)
    started = []

    def push(p, phase, offset, src, dst):
        axis = ORDERS[p][phase]
        slot = p * 9 + phase * 3 + offset - 1
        copy = remote(
            src, dst, ring_send.at[slot], ring_recv.at[slot],
            place.partner(axis, place.ahead(axis, offset)),
        )
        copy.start()
        started.append(copy)
        return copy

    first = {}
    for offset in (2, 1, 3):
        for p in range(3):
            left, right = part(p, place.ahead(ORDERS[p][0], offset))
            send1[p][offset - 1, :, :half] = left.astype(BF16)
            send1[p][offset - 1, :, half:] = right.astype(BF16)
            first[p, offset] = push(p, 0, offset, send1[p].at[offset - 1], recv1[p].at[offset - 1])
    for p in range(3):
        left, right = part(p, place.at[ORDERS[p][0]])
        acc1[p][:, :half] = left
        acc1[p][:, half:] = right
    second = {}
    for p in range(3):
        for offset in (1, 2, 3):
            first[p, offset].wait_recv()
        acc1[p][...] += (
            recv1[p][0].astype(F32) + recv1[p][1].astype(F32) + recv1[p][2].astype(F32)
        )
        for offset in (2, 1, 3):
            dest = place.ahead(ORDERS[p][1], offset)
            send2[p][offset - 1] = acc1[p][pl.ds(pl.multiple_of(dest * 64, 64), 64)].astype(BF16)
            second[p, offset] = push(p, 1, offset, send2[p].at[offset - 1], recv2[p].at[offset - 1])
    third = {}
    for p in range(3):
        for offset in (1, 2, 3):
            second[p, offset].wait_recv()
        own = acc1[p][pl.ds(pl.multiple_of(place.at[ORDERS[p][1]] * 64, 64), 64)]
        acc2[p][...] = own + (
            recv2[p][0].astype(F32) + recv2[p][1].astype(F32) + recv2[p][2].astype(F32)
        )
        for offset in (2, 1, 3):
            dest = place.ahead(ORDERS[p][2], offset)
            src = acc2[p].at[pl.ds(pl.multiple_of(dest * 16, 16), 16)]
            third[p, offset] = push(p, 2, offset, src, recv3[p].at[offset - 1])
    last = []
    for p in range(3):
        for offset in (1, 2, 3):
            third[p, offset].wait_recv()
        own = acc2[p][pl.ds(pl.multiple_of(place.at[ORDERS[p][2]] * 16, 16), 16)]
        fin[p][...] = own + recv3[p][0] + recv3[p][1] + recv3[p][2]
        copy = remote(
            fin[p].at[pl.ds(pl.multiple_of((1 - core) * 8, 8), 8)], oth[p],
            last_send.at[p], last_recv.at[p], place.pair(),
        )
        copy.start()
        last.append(copy)
    keep = pl.ds(pl.multiple_of(core * 8, 8), 8)

    def both(own, other):
        return jnp.where(core == 0, own, other), jnp.where(core == 0, other, own)

    for p in range(3):
        last[p].wait_recv()
        low, high = both(fin[p][keep, :half], oth[p][:, :half])
        g_qkv[:, p * 1024 : p * 1024 + half] = low
        g_qkv[:, p * 1024 + half : p * 1024 + 2 * half] = high
        if p == 0:
            g_out[...] = fin[p][keep, half:] + oth[p][:, half:]
        else:
            low, high = both(fin[p][keep, half:], oth[p][:, half:])
            g_o[:, (p - 1) * 256 : p * 256] = low
            g_o[:, half + (p - 1) * 256 : half + p * 256] = high
    for copy in pair + started + last:
        copy.wait_send()


def reduce_terms(xn, dqkv, att, daf, aft, crps):
    rows = xn.shape[0]
    vmem = pl.BlockSpec(memory_space=pltpu.VMEM)
    scratch = [
        pltpu.VMEM((rows, 1024), BF16),
        pltpu.VMEM((rows, 1024), BF16),
        *[pltpu.VMEM((2 * rows, 512), BF16)] * 4,
        *[pltpu.VMEM((1024, 2 * rows), BF16)] * 5,
        pltpu.VMEM((1024, rows), BF16),
        *[pltpu.VMEM((3, 256, w), BF16) for w in WIDTHS],
        *[pltpu.VMEM((3, 256, w), BF16) for w in WIDTHS],
        *[pltpu.VMEM((256, w), F32) for w in WIDTHS],
        *[pltpu.VMEM((3, 64, w), BF16) for w in WIDTHS],
        *[pltpu.VMEM((3, 64, w), BF16) for w in WIDTHS],
        *[pltpu.VMEM((64, w), F32) for w in WIDTHS],
        *[pltpu.VMEM((3, 16, w), F32) for w in WIDTHS],
        *[pltpu.VMEM((16, w), F32) for w in WIDTHS],
        *[pltpu.VMEM((8, w), F32) for w in WIDTHS],
        pltpu.SemaphoreType.DMA((6,)),
        pltpu.SemaphoreType.DMA((6,)),
        pltpu.SemaphoreType.DMA((27,)),
        pltpu.SemaphoreType.DMA((27,)),
        pltpu.SemaphoreType.DMA((3,)),
        pltpu.SemaphoreType.DMA((3,)),
    ]
    return pl.pallas_call(
        reduce_kernel,
        out_shape=(
            jax.ShapeDtypeStruct((8, 3072), F32),
            jax.ShapeDtypeStruct((8, 1024), F32),
            jax.ShapeDtypeStruct((8, 128), F32),
        ),
        in_specs=[vmem] * 6,
        out_specs=[vmem] * 3,
        scratch_shapes=scratch,
        compiler_params=pltpu.CompilerParams(
            collective_id=0, has_side_effects=True, vmem_limit_bytes=48 * 1024 * 1024
        ),
    )(xn, dqkv, att, daf, aft, crps)


def extended(value, sides, width):
    for axis, dim in sides:
        count, length = (lax.axis_size(axis), value.shape[dim])
        up = [(i, (i + 1) % count) for i in range(count - 1)]
        down = [(j, i) for i, j in up]
        last = lax.slice_in_dim(value, length - width, length, axis=dim)
        leading = lax.slice_in_dim(value, 0, width, axis=dim)
        before = lax.ppermute(last, axis, up)
        after = lax.ppermute(leading, axis, down)
        value = jnp.concatenate([before, value, after], axis=dim)
    return value


def crps_terms(own, every, target_part, weight_part, total):
    first = jnp.sign(own - target_part[None])
    pair = jnp.sum(jnp.sign(own[:, None] - every[None]), axis=1)
    return weight_part[None, None, :] * (first - pair / (total - 1))


def on_device(latent, predictions, target, area_weight, slab_count, w_qkv, w_o, w_out):
    members_here, points, width = latent.shape
    place = jnp.arange(points)
    live = place < slab_count[0]
    pweight = jnp.where(live, area_weight, jnp.zeros_like(area_weight))
    total = lax.axis_size("member") * members_here
    every = lax.all_gather(predictions, "member", axis=0, tiled=True)
    crps = crps_terms(predictions, every, target, pweight, total)
    xf = latent.astype(jnp.float32)
    mean = jnp.mean(xf, axis=-1, keepdims=True)
    cent = xf - mean
    var = jnp.mean(cent * cent, axis=-1, keepdims=True)
    rstd = lax.rsqrt(var + 1e-05)
    norm = cent * rstd
    xn = norm.astype(jnp.bfloat16)
    qkv = jnp.einsum("mpd,de->mpe", xn, w_qkv, preferred_element_type=jnp.float32).astype(
        jnp.bfloat16
    )
    query = qkv[..., :width]
    keyval = qkv[..., width:]
    wide = extended(keyval, (("space", 1),), BLOCK)
    nblk = points // BLOCK
    heads = width // HEAD_DIM
    scale = HEAD_DIM ** (-0.5)
    blocks = wide.reshape(members_here, nblk + 2, BLOCK, 2 * width)
    window = jnp.concatenate([blocks[:, :-2], blocks[:, 1:-1], blocks[:, 2:]], axis=2)
    qh = query.reshape(members_here, nblk, BLOCK, heads, HEAD_DIM)
    kh = window[..., :width].reshape(members_here, nblk, 3 * BLOCK, heads, HEAD_DIM)
    vh = window[..., width:].reshape(members_here, nblk, 3 * BLOCK, heads, HEAD_DIM)
    slab = lax.axis_index("space")
    final = lax.axis_size("space") - 1
    ext = jnp.arange(nblk)[:, None] + (jnp.arange(3 * BLOCK) // BLOCK)[None, :]
    valid = ((ext >= 1) | (slab > 0)) & ((ext <= nblk) | (slab < final))
    scores = jnp.einsum("mnqhd,mnkhd->mnhqk", qh, kh, preferred_element_type=jnp.float32) * scale
    scores = jnp.where(valid[None, :, None, None, :], scores, -1e30)
    prob = jax.nn.softmax(scores, axis=-1)
    prob_b = prob.astype(jnp.bfloat16)
    attended = jnp.einsum("mnhqk,mnkhd->mnqhd", prob_b, vh, preferred_element_type=jnp.float32)
    attended = attended.astype(jnp.bfloat16).reshape(members_here, points, width)
    after = (
        xf + jnp.einsum("mpd,de->mpe", attended, w_o, preferred_element_type=jnp.float32)
    ).astype(jnp.bfloat16)
    crps_b = crps.astype(jnp.bfloat16)
    dafter = jnp.einsum("mcp,dc->mpd", crps_b, w_out, preferred_element_type=jnp.float32)
    dafter_b = dafter.astype(jnp.bfloat16)
    dattend = jnp.einsum("mpe,de->mpd", dafter_b, w_o, preferred_element_type=jnp.float32).astype(
        jnp.bfloat16
    )
    dattend = dattend.reshape(members_here, nblk, BLOCK, heads, HEAD_DIM)
    dprob = jnp.einsum("mnqhd,mnkhd->mnhqk", dattend, vh, preferred_element_type=jnp.float32)
    dval = jnp.einsum("mnhqk,mnqhd->mnkhd", prob_b, dattend, preferred_element_type=jnp.float32)
    delta = jnp.sum(dprob * prob, axis=-1, keepdims=True)
    dscore = (prob * (dprob - delta) * scale).astype(jnp.bfloat16)
    dquery = jnp.einsum("mnhqk,mnkhd->mnqhd", dscore, kh, preferred_element_type=jnp.float32)
    dquery = dquery.reshape(members_here, points, width)
    dkey = jnp.einsum("mnhqk,mnqhd->mnkhd", dscore, qh, preferred_element_type=jnp.float32)
    dwin = jnp.concatenate(
        [
            dkey.reshape(members_here, nblk, 3 * BLOCK, width),
            dval.reshape(members_here, nblk, 3 * BLOCK, width),
        ],
        axis=-1,
    )
    dwin = dwin.reshape(members_here, nblk, 3, BLOCK, 2 * width)
    dwide = jnp.pad(dwin[:, :, 0], ((0, 0), (0, 2), (0, 0), (0, 0)))
    dwide = dwide + jnp.pad(dwin[:, :, 1], ((0, 0), (1, 1), (0, 0), (0, 0)))
    dwide = dwide + jnp.pad(dwin[:, :, 2], ((0, 0), (2, 0), (0, 0), (0, 0)))
    owned = dwide[:, 1:-1].reshape(members_here, points, 2 * width)
    sides = jnp.concatenate([dwide[:, 0], dwide[:, -1]], axis=1)
    returned = extended(sides, (("space", 1),), BLOCK)
    owned = owned.at[:, :BLOCK].add(returned[:, :BLOCK])
    owned = owned.at[:, points - BLOCK :].add(returned[:, 3 * BLOCK :])
    dqkv = jnp.concatenate([dquery, owned], axis=-1).astype(jnp.bfloat16)
    dnorm = jnp.einsum("mpe,de->mpd", dqkv, w_qkv, preferred_element_type=jnp.float32)
    dlayer = rstd * (
        dnorm
        - jnp.mean(dnorm, axis=-1, keepdims=True)
        - norm * jnp.mean(dnorm * norm, axis=-1, keepdims=True)
    )
    grad_latent = (dafter + dlayer).astype(jnp.bfloat16)
    rows = members_here * points
    channels = crps_b.shape[1]
    crps_rows = jnp.pad(crps_b.transpose(0, 2, 1).reshape(rows, channels), ((0, 0), (0, 128 - channels)))
    grad_qkv, grad_o, grad_out = reduce_terms(
        xn.reshape(rows, width), dqkv.reshape(rows, 3 * width), attended.reshape(rows, width),
        dafter_b.reshape(rows, width), after.reshape(rows, width), crps_rows,
    )
    grad_out = grad_out[:, :channels]
    return (grad_latent, grad_qkv, grad_o, grad_out)


def solution(mesh):
    placed = (
        P("member", "space", None),
        P("member", None, "space"),
        P(None, "space"),
        P("space"),
        P("space"),
        P(),
        P(),
        P(),
    )
    return jax.shard_map(
        on_device,
        mesh=mesh,
        in_specs=placed,
        out_specs=(
            P("member", "space", None),
            P(("member", "space"), None),
            P(("member", "space"), None),
            P(("member", "space"), None),
        ),
        check_vma=False,
    )
```

```python
from types import SimpleNamespace

import jax
import jax.numpy as jnp
from jax import lax
from jax.experimental import pallas as pl
from jax.experimental.pallas import tpu as pltpu
from jax.sharding import PartitionSpec as P

RING = 4
MEMBERS_DEV = 2
ROWS = 256
WIDTH = 1024
HALF = 512
GROUP = 256
CHANNEL_GROUP = 16
LOG2E = 1.4426950408889634
F32 = jnp.float32
BF16 = jnp.bfloat16
MESH = pl.DeviceIdType.MESH

ORDERS = (("x", "y", "z"), ("y", "z", "x"), ("z", "x", "y"))
WIDTHS = ((384, 384, 384), (384, 384, 256))


class Place:
    def __init__(self):
        self.member = lax.axis_index("member")
        self.space = lax.axis_index("space")
        self.core = self.space % 2
        z_lo = (self.space // 2) % 2
        z_hi = self.member % 2
        self.at = {"x": self.space // 4, "y": self.member // 2, "z": z_hi * 2 + z_lo}

    def partner(self, axis, index):
        if axis == "x":
            return (self.member, index * 4 + self.space % 4)
        if axis == "y":
            return (index * 2 + self.member % 2, self.space)
        member = (self.member // 2) * 2 + index // 2
        return (member, (self.space // 4) * 4 + (index % 2) * 2 + self.core)

    def pair(self):
        return (self.member, self.space + 1 - 2 * self.core)

    def right(self):
        return (self.member, (self.space + 1) % 16)

    def left(self):
        return (self.member, (self.space + 15) % 16)

    def across(self, axis, offset):
        member, space = self.partner(axis, self.ahead(axis, offset))
        return (member, space + 1 - 2 * self.core)

    def ahead(self, axis, offset):
        return (self.at[axis] + offset) % RING


def chunk_order(order):
    where = []
    for y in range(4):
        for z_hi in range(2):
            for x in range(4):
                for z_lo in range(2):
                    digit = {"x": x, "y": y, "z": z_hi * 2 + z_lo}
                    a, b, c = (digit[name] for name in order)
                    where.append(a * 16 + b * 4 + c)
    return where


def remote(src, dst, send, recv, device):
    return pltpu.make_async_remote_copy(
        src_ref=src, dst_ref=dst, send_sem=send, recv_sem=recv, device_id=device, device_id_type=MESH
    )


def dot(a, b):
    return jnp.dot(a, b, preferred_element_type=F32)


def dot_nt(a, b):
    return lax.dot_general(a, b, (((1,), (1,)), ((), ())), preferred_element_type=F32)


def sign_of(a, b):
    one = jnp.float32(1.0)
    zero = jnp.float32(0.0)
    return jnp.where(a > b, one, zero) - jnp.where(a < b, one, zero)


def scratch():
    vmem = pltpu.VMEM
    dma = pltpu.SemaphoreType.DMA
    block3 = vmem((3, ROWS, WIDTH), BF16)
    rows_b = vmem((ROWS, WIDTH), BF16)
    rows_f = vmem((ROWS, WIDTH), F32)
    factor = vmem((2 * ROWS, HALF), BF16)
    turned = vmem((WIDTH, 2 * ROWS), BF16)

    def waves(*shape, dtype):
        return [[vmem((*shape, w), dtype) for w in widths] for widths in WIDTHS]

    return dict(
        w_in=vmem((WIDTH, 3 * WIDTH), BF16),
        w_back=vmem((WIDTH, WIDTH), BF16),
        w_dec=vmem((128, WIDTH), BF16),
        lat=block3, xn=block3, qx=block3, kx=block3, vx=block3, dx=block3,
        norm=rows_f, daf=rows_f, dk_acc=rows_f, dv_acc=rows_f, dnorm=rows_f,
        rstd=vmem((ROWS, 128), F32),
        daf_b=block3,
        att=rows_b, att_o=rows_b,
        dqkv=vmem((ROWS, 3 * WIDTH), BF16),
        mask=vmem((4 * 128, GROUP), BF16),
        stat=vmem((4, 8, 512), F32),
        stat_n=vmem((2, 4, 8, 512), F32),
        pred_p=vmem((2, 128, 128), F32),
        targ_p=vmem((128, 128), F32),
        pred_g=vmem((8, 2, CHANNEL_GROUP, 128), F32),
        crps_g=vmem((8, 2, CHANNEL_GROUP, 128), BF16),
        cr=vmem((3, 2, 128, 128), BF16),
        cr_rows=vmem((ROWS, 128), BF16),
        d_q=factor, d_k=factor, d_v=factor, d_o=factor,
        xt=[turned] * 3,
        at=[turned] * 2,
        ft=vmem((WIDTH, ROWS), BF16),
        send1=waves(6, 128, dtype=BF16),
        recv1=waves(6, 128, dtype=BF16),
        hold=waves(2, 128, dtype=F32),
        acc1=waves(256, dtype=F32),
        send2=waves(3, 64, dtype=BF16),
        recv2=waves(3, 64, dtype=BF16),
        acc2=waves(64, dtype=F32),
        recv3=waves(7, 8, dtype=F32),
        load=dma((5,)),
        halo_s=dma((2,)), halo_r=dma((2,)),
        pred_s=dma((7,)), pred_r=dma((7,)),
        back_s=dma((7,)), back_r=dma((7,)),
        crh_s=dma((2,)), crh_r=dma((2,)),
        sth_s=dma((2,)), sth_r=dma((2,)),
        pair_s=dma((5,)), pair_r=dma((5,)),
        ring_s=dma((96,)), ring_r=dma((96,)),
    )


SHAPES, TREE = jax.tree.flatten(scratch())


def kernel(
    latent, predictions, target, area_weight, slab_count, w_qkv, w_o, w_out, g_latent, g_qkv, g_o, g_out, *buffers
):
    r = SimpleNamespace(**jax.tree.unflatten(TREE, buffers))
    place = Place()
    core, member, slab = place.core, place.member, place.space
    sent = []

    def start(copy):
        copy.start()
        sent.append(copy)
        return copy

    load = r.load
    loads = [
        pltpu.make_async_copy(latent, r.lat.at[1], load.at[0]),
        pltpu.make_async_copy(w_qkv.at[:, pl.ds(0, WIDTH)], r.w_in.at[:, pl.ds(0, WIDTH)], load.at[1]),
        pltpu.make_async_copy(w_qkv.at[:, pl.ds(WIDTH, WIDTH)], r.w_in.at[:, pl.ds(WIDTH, WIDTH)], load.at[2]),
        pltpu.make_async_copy(
            w_qkv.at[:, pl.ds(2 * WIDTH, WIDTH)], r.w_in.at[:, pl.ds(2 * WIDTH, WIDTH)], load.at[3]
        ),
        pltpu.make_async_copy(w_o, r.w_back, load.at[4]),
    ]
    for copy in loads:
        copy.start()

    barrier = pltpu.get_barrier_semaphore()
    greeted = [((member + o) % 8, slab) for o in range(1, 8)]
    greeted += [place.partner(axis, place.ahead(axis, o)) for axis in ("x", "z") for o in (1, 2, 3)]
    greeted += [place.right(), place.left()]
    greeted += [place.across(axis, o) for axis in ("x", "y", "z") for o in (1, 2, 3)]
    for device in greeted:
        pl.semaphore_signal(barrier, inc=1, device_id=device, device_id_type=MESH)

    r.pred_p[...] = jnp.zeros((2, 128, 128), F32)
    r.targ_p[...] = jnp.zeros((128, 128), F32)
    r.w_dec[...] = jnp.zeros((128, WIDTH), BF16)
    channels = target.shape[0]
    for m in range(MEMBERS_DEV):
        r.pred_p[m, :channels, :] = predictions[:, m, :]
    r.targ_p[:channels, :] = target[...]
    r.w_dec[:channels, :] = w_out[...]
    head_row = lax.broadcasted_iota(jnp.int32, (512, GROUP), 0) // 128
    head_col = lax.broadcasted_iota(jnp.int32, (512, GROUP), 1) // 64
    r.mask[...] = jnp.where(head_row == head_col, jnp.float32(1.0), jnp.float32(0.0)).astype(BF16)

    pl.semaphore_wait(barrier, len(greeted))

    pred_copies = []
    for o in range(1, 8):
        dest = (member + o) % 8
        pred_copies.append(start(remote(
            r.pred_p.at[:, pl.ds(pl.multiple_of(dest * CHANNEL_GROUP, CHANNEL_GROUP), CHANNEL_GROUP)],
            r.pred_g.at[member], r.pred_s.at[o - 1], r.pred_r.at[o - 1], (dest, slab),
        )))
    halo = [
        start(remote(latent, r.lat.at[0], r.halo_s.at[0], r.halo_r.at[0], place.right())),
        start(remote(latent, r.lat.at[2], r.halo_s.at[1], r.halo_r.at[1], place.left())),
    ]

    def normalise(block, keep):
        xf = r.lat[block].astype(F32)
        mean = jnp.mean(xf, axis=-1, keepdims=True)
        cent = xf - mean
        var = jnp.mean(cent * cent, axis=-1, keepdims=True)
        rstd = lax.rsqrt(var + 1e-05)
        norm = cent * rstd
        r.xn[block] = norm.astype(BF16)
        if keep:
            r.norm[...] = norm
            r.rstd[...] = jnp.broadcast_to(rstd, (ROWS, 128))

    def project(block):
        for j in range(6):
            piece = dot(r.xn[block], r.w_in[:, j * HALF : (j + 1) * HALF]).astype(BF16)
            at = slice((j % 2) * HALF, (j % 2 + 1) * HALF)
            if j < 2:
                r.qx[block, :, at] = piece * jnp.bfloat16(0.125)
            elif j < 4:
                r.kx[block, :, at] = piece
            else:
                r.vx[block, :, at] = piece

    loads[0].wait()
    normalise(1, True)
    for copy in loads[1:]:
        copy.wait()
    project(1)

    r.pred_g[member] = r.pred_p[:, pl.ds(pl.multiple_of(member * CHANNEL_GROUP, CHANNEL_GROUP), CHANNEL_GROUP), :]
    for copy in pred_copies:
        copy.wait_recv()
    y = [r.pred_g[i // 2, i % 2] for i in range(16)]
    pair_sum = [jnp.zeros((CHANNEL_GROUP, 128), F32) for _ in range(16)]
    for i in range(16):
        for k in range(i + 1, 16):
            s = sign_of(y[i], y[k])
            pair_sum[i] = pair_sum[i] + s
            pair_sum[k] = pair_sum[k] - s
    point = lax.broadcasted_iota(jnp.int32, (1, 128), 1)
    pweight = jnp.where(point < slab_count[0], area_weight[...], jnp.zeros((1, 128), F32))
    truth = r.targ_p[pl.ds(pl.multiple_of(member * CHANNEL_GROUP, CHANNEL_GROUP), CHANNEL_GROUP), :]
    for i in range(16):
        crps = pweight * (sign_of(y[i], truth) - pair_sum[i] / 15.0)
        r.crps_g[i // 2, i % 2] = crps.astype(BF16)
    own_group = pl.ds(pl.multiple_of(member * CHANNEL_GROUP, CHANNEL_GROUP), CHANNEL_GROUP)
    back_copies = []
    for o in range(1, 8):
        dest = (member + o) % 8
        back_copies.append(start(remote(
            r.crps_g.at[dest], r.cr.at[1, :, own_group], r.back_s.at[o - 1], r.back_r.at[o - 1], (dest, slab)
        )))
    r.cr[1, :, own_group, :] = r.crps_g[member]

    near, far = 2 - 2 * core, 2 * core
    near_i, far_i = 1 - core, core

    def arrived(src, dst, send, recv, side, i):
        remote(src, dst.at[side], send.at[i], recv.at[i], place.pair()).wait_recv()

    arrived(latent, r.lat, r.halo_s, r.halo_r, near, near_i)
    normalise(near, False)
    project(near)

    for copy in back_copies:
        copy.wait_recv()
    crh = [
        start(remote(r.cr.at[1], r.cr.at[0], r.crh_s.at[0], r.crh_r.at[0], place.right())),
        start(remote(r.cr.at[1], r.cr.at[2], r.crh_s.at[1], r.crh_r.at[1], place.left())),
    ]

    def decode(block):
        for m in range(2):
            turned = r.cr[block, m].T
            value = dot(turned, r.w_dec[...])
            at = slice(m * 128, m * 128 + 128)
            r.daf_b[block, at, :] = value.astype(BF16)
            if isinstance(block, int):
                r.daf[at, :] = value
                r.cr_rows[at, :] = turned

    def attend_back(block):
        for j in range(4):
            at = slice(j * GROUP, (j + 1) * GROUP)
            r.dx[block, :, at] = dot_nt(r.daf_b[block], r.w_back[at, :]).astype(BF16)

    def lay(value, targets, column):
        turned = value.T
        for ref, order in targets:
            for chunk, spot in enumerate(chunk_order(order)):
                ref[spot * 16 : spot * 16 + 16, column : column + ROWS] = turned[chunk * 16 : chunk * 16 + 16]

    xts = [(r.xt[0], ORDERS[0]), (r.xt[1], ORDERS[1]), (r.xt[2], ORDERS[2])]
    ats = [(r.at[0], ORDERS[1]), (r.at[1], ORDERS[2])]

    decode(1)
    theirs = pl.multiple_of((1 - core) * HALF, HALF)
    high_rows = pl.ds(ROWS, ROWS)

    def give(i, src, dst):
        return start(remote(src, dst, r.pair_s.at[i], r.pair_r.at[i], place.pair()))

    pair_o = give(0, r.daf_b.at[1, :, pl.ds(theirs, HALF)], r.d_o.at[high_rows])
    attend_back(1)
    arrived(r.cr.at[1], r.cr, r.crh_s, r.crh_r, near, near_i)
    decode(near)
    attend_back(near)
    lay(r.xn[1], xts, 0)
    lay(r.xn[near], xts, ROWS)
    arrived(r.cr.at[1], r.cr, r.crh_s, r.crh_r, far, far_i)
    decode(far)
    attend_back(far)
    arrived(latent, r.lat, r.halo_s, r.halo_r, far, far_i)
    normalise(far, False)
    project(far)

    edge = [
        jnp.where(slab > 0, jnp.float32(0.0), jnp.float32(-1e30)),
        jnp.where(slab < 15, jnp.float32(0.0), jnp.float32(-1e30)),
    ]

    def spread(block):
        return jnp.concatenate([block, block, block, block], axis=0) * r.mask[...]

    def gather_heads(value):
        return jnp.concatenate(
            [value[h * 64 : (h + 1) * 64, h * 128 : (h + 1) * 128] for h in range(4)], axis=0
        ).T

    def own_queries(g, carry):
        cols = pl.ds(pl.multiple_of(g * GROUP, GROUP), GROUP)
        for m in range(2):
            rows = slice(m * 128, (m + 1) * 128)
            keys = jnp.concatenate([r.kx[b, rows, cols] for b in range(3)], axis=0)
            values = jnp.concatenate([r.vx[b, rows, cols] for b in range(3)], axis=0)
            q_b = spread(r.qx[1, rows, cols])
            d_b = spread(r.dx[1, rows, cols])
            scores = dot_nt(keys, q_b)
            scores = jnp.concatenate([scores[:128] + edge[0], scores[128:256], scores[256:] + edge[1]], axis=0)
            top = jnp.max(scores, axis=0, keepdims=True) * LOG2E
            e = jnp.exp2(scores * LOG2E - top)
            total = jnp.sum(e, axis=0, keepdims=True)
            prob = e * (1.0 / total)
            prob_b = prob.astype(BF16)
            dprob = dot_nt(values, d_b)
            delta = jnp.sum(dprob * prob, axis=0, keepdims=True)
            dscore = (prob * (dprob - delta)).astype(BF16)
            r.att[rows, cols] = gather_heads(dot(values.T, prob_b)).astype(BF16)
            r.dqkv[rows, cols] = (gather_heads(dot(keys.T, dscore)) * 0.125).astype(BF16)
            r.dk_acc[rows, cols] = dot(dscore[128:256], q_b)
            r.dv_acc[rows, cols] = dot(prob_b[128:256], d_b)
            r.stat[g, 2 * m : 2 * m + 1, :] = top + jnp.log2(total)
            r.stat[g, 2 * m + 1 : 2 * m + 2, :] = delta
        return carry

    r.stat[...] = jnp.zeros((4, 8, 512), F32)
    lax.fori_loop(0, 4, own_queries, 0)
    sth = [
        start(remote(r.stat, r.stat_n.at[0], r.sth_s.at[0], r.sth_r.at[0], place.right())),
        start(remote(r.stat, r.stat_n.at[1], r.sth_s.at[1], r.sth_r.at[1], place.left())),
    ]
    pair_a = give(1, r.att, r.att_o)
    pair_q = give(2, r.dqkv.at[:, pl.ds(theirs, HALF)], r.d_q.at[high_rows])

    def mine(ref, at, begin):
        return jnp.where(core == 0, ref[at, begin : begin + HALF], ref[at, begin + HALF : begin + 2 * HALF])

    r.d_o[:ROWS] = mine(r.daf_b.at[1], slice(0, ROWS), 0)
    r.d_q[:ROWS] = mine(r.dqkv, slice(0, ROWS), 0)

    after = r.lat[1].astype(F32) + dot(r.att[...], r.w_back[...])
    lay(after.astype(BF16), [(r.ft, ORDERS[2])], 0)
    lay(r.att[...], ats, 0)
    pair_a.wait_recv()
    lay(r.att_o[...], ats, ROWS)

    def terms(wave, p, dest):
        at = pl.ds(pl.multiple_of(dest * 256, 256), 256)
        if wave == 0:
            if p == 0:
                return [dot(r.xt[0][at, :], r.d_q[:, :384])]
            if p == 1:
                return [dot(r.xt[1][at, :], r.d_q[:, 384:]), dot(r.at[0][at, :], r.d_o[:, :256])]
            return [dot(r.at[1][at, :], r.d_o[:, 256:]), dot(r.ft[at, :], r.cr_rows[...])]
        if p == 0:
            return [dot(r.xt[0][at, :], r.d_k[:, :384])]
        if p == 1:
            return [dot(r.xt[1][at, :], r.d_k[:, 384:]), dot(r.xt[1][at, :], r.d_v[:, :256])]
        return [dot(r.xt[2][at, :], r.d_v[:, 256:])]

    def push(wave, p, slot, src, dst, device):
        slot = (wave * 3 + p) * 16 + slot
        return start(remote(src, dst, r.ring_s.at[slot], r.ring_r.at[slot], device))

    def neighbour(p, phase, offset):
        axis = ORDERS[p][phase]
        return place.partner(axis, place.ahead(axis, offset))

    def put(ref, index, values, dtype, rows=slice(None)):
        begin = 0
        for value in values:
            end = begin + value.shape[1]
            ref[index, rows, begin:end] = value.astype(dtype)
            begin = end

    def first(wave):
        copies = {}

        def go(p, slot, offset):
            copies[p, slot] = push(
                wave, p, slot, r.send1[wave][p].at[slot], r.recv1[wave][p].at[slot], neighbour(p, 0, offset)
            )

        for p in range(3):
            values = terms(wave, p, place.ahead(ORDERS[p][0], 2))
            put(r.send1[wave][p], 0, [v[:128] for v in values], BF16)
            put(r.send1[wave][p], 1, [v[128:] for v in values], BF16)
            go(p, 0, 1)
            go(p, 1, 3)
        for p in range(3):
            values = terms(wave, p, place.ahead(ORDERS[p][0], 1))
            put(r.send1[wave][p], 2, [v[128:] for v in values], BF16)
            put(r.hold[wave][p], 0, [v[:128] for v in values], F32)
            go(p, 2, 1)
            values = terms(wave, p, place.ahead(ORDERS[p][0], 3))
            put(r.send1[wave][p], 3, [v[:128] for v in values], BF16)
            put(r.hold[wave][p], 1, [v[128:] for v in values], F32)
            go(p, 3, 3)
        return copies

    def relay(wave, copies):
        for p in range(3):
            for half, offset in ((0, 1), (1, 3)):
                copies[p, half].wait_recv()
                r.send1[wave][p][4 + half] = (r.hold[wave][p][half] + r.recv1[wave][p][half].astype(F32)).astype(BF16)
                copies[p, 4 + half] = push(
                    wave, p, 4 + half, r.send1[wave][p].at[4 + half], r.recv1[wave][p].at[4 + half],
                    neighbour(p, 0, offset),
                )

    def own_terms(wave):
        for p in range(3):
            begin = 0
            for value in terms(wave, p, place.at[ORDERS[p][0]]):
                end = begin + value.shape[1]
                r.acc1[wave][p][:, begin:end] = value
                begin = end

    def second(wave, arrivals):
        copies = {}
        for p in range(3):
            acc, came = r.acc1[wave][p], r.recv1[wave][p]
            for slot in (2, 3, 4, 5):
                arrivals[p, slot].wait_recv()
            acc[:128] += came[3].astype(F32) + came[4].astype(F32)
            acc[128:] += came[2].astype(F32) + came[5].astype(F32)
            for offset in (2, 1, 3):
                dest = place.ahead(ORDERS[p][1], offset)
                r.send2[wave][p][offset - 1] = acc[pl.ds(pl.multiple_of(dest * 64, 64), 64), :].astype(BF16)
                copies[p, offset] = push(
                    wave, p, 5 + offset, r.send2[wave][p].at[offset - 1], r.recv2[wave][p].at[offset - 1],
                    neighbour(p, 1, offset),
                )
        return copies

    def third(wave, arrivals):
        copies = []
        for p in range(3):
            for offset in (1, 2, 3):
                arrivals[p, offset].wait_recv()
            own = r.acc1[wave][p][pl.ds(pl.multiple_of(place.at[ORDERS[p][1]] * 64, 64), 64), :]
            came = r.recv2[wave][p]
            r.acc2[wave][p][...] = own + (came[0].astype(F32) + came[1].astype(F32) + came[2].astype(F32))
            for offset in (2, 1, 3, 0):
                dest = place.ahead(ORDERS[p][2], offset)
                device = neighbour(p, 2, offset)
                for other in ((0, 1) if offset else (1,)):
                    side = core if other == 0 else 1 - core
                    slot = 3 + offset if other else offset - 1
                    src = r.acc2[wave][p].at[pl.ds(pl.multiple_of(dest * 16 + side * 8, 8), 8)]
                    to = (device[0], device[1] + (side - core))
                    copies.append(push(wave, p, 9 + slot, src, r.recv3[wave][p].at[slot], to))
        return copies

    def finish(wave, arrivals):
        for copy in arrivals:
            copy.wait_recv()
        own, other = [], []
        for p in range(3):
            came = r.recv3[wave][p]
            at = pl.ds(pl.multiple_of(place.at[ORDERS[p][2]] * 16 + core * 8, 8), 8)
            own.append(r.acc2[wave][p][at, :] + came[0] + came[1] + came[2])
            other.append(came[3] + came[4] + came[5] + came[6])
        return own, other

    def place_both(out, begin, own, other):
        width = own.shape[1]
        out[:, begin : begin + width] = jnp.where(core == 0, own, other)
        out[:, begin + HALF : begin + HALF + width] = jnp.where(core == 0, other, own)

    pair_o.wait_recv()
    pair_q.wait_recv()
    arrive0 = first(0)
    own_terms(0)

    for copy in sth:
        copy.wait_recv()

    def other_queries(g, carry):
        cols = pl.ds(pl.multiple_of(g * GROUP, GROUP), GROUP)
        for m in range(2):
            rows = slice(m * 128, (m + 1) * 128)
            keys = r.kx[1, rows, cols]
            values = r.vx[1, rows, cols]
            dk = r.dk_acc[rows, cols]
            dv = r.dv_acc[rows, cols]
            for side in range(2):
                q_b = spread(r.qx[2 * side, rows, cols])
                d_b = spread(r.dx[2 * side, rows, cols])
                lse = r.stat_n[side, g, 2 * m : 2 * m + 1, :]
                delta = r.stat_n[side, g, 2 * m + 1 : 2 * m + 2, :]
                prob = jnp.exp2(dot_nt(keys, q_b) * LOG2E - (lse - edge[side]))
                dscore = (prob * (dot_nt(values, d_b) - delta)).astype(BF16)
                dk += dot(dscore, q_b)
                dv += dot(prob.astype(BF16), d_b)
            r.dqkv[rows, pl.ds(pl.multiple_of(WIDTH + g * GROUP, GROUP), GROUP)] = dk.astype(BF16)
            r.dqkv[rows, pl.ds(pl.multiple_of(2 * WIDTH + g * GROUP, GROUP), GROUP)] = dv.astype(BF16)
        return carry

    lax.fori_loop(0, 2, other_queries, 0)
    relay(0, arrive0)
    lax.fori_loop(2, 4, other_queries, 0)
    pair_k = give(3, r.dqkv.at[:, pl.ds(pl.multiple_of(WIDTH + theirs, HALF), HALF)], r.d_k.at[high_rows])
    pair_v = give(4, r.dqkv.at[:, pl.ds(pl.multiple_of(2 * WIDTH + theirs, HALF), HALF)], r.d_v.at[high_rows])
    r.d_k[:ROWS] = mine(r.dqkv, slice(0, ROWS), WIDTH)
    r.d_v[:ROWS] = mine(r.dqkv, slice(0, ROWS), 2 * WIDTH)
    arrive0 = second(0, arrive0)
    pair_k.wait_recv()
    pair_v.wait_recv()
    arrive1 = first(1)
    arrive0 = third(0, arrive0)
    own_terms(1)
    relay(1, arrive1)

    for j in range(4):
        at = slice(j * GROUP, (j + 1) * GROUP)
        r.dnorm[:, at] = dot_nt(r.dqkv[...], r.w_in[at, :])
    dnorm = r.dnorm[...]
    norm = r.norm[...]
    dlayer = r.rstd[:, :1] * (
        dnorm
        - jnp.mean(dnorm, axis=-1, keepdims=True)
        - norm * jnp.mean(dnorm * norm, axis=-1, keepdims=True)
    )
    g_latent[...] = (r.daf[...] + dlayer).astype(BF16)

    arrive1 = second(1, arrive1)
    own, other = finish(0, arrive0)
    place_both(g_qkv, 0, own[0], other[0])
    place_both(g_qkv, 384, own[1][:, :128], other[1][:, :128])
    place_both(g_o, 0, own[1][:, 128:], other[1][:, 128:])
    place_both(g_o, 256, own[2][:, :256], other[2][:, :256])
    total = own[2][:, 256:] + other[2][:, 256:]
    g_out[...] = total[:, :channels]

    arrive1 = third(1, arrive1)
    own, other = finish(1, arrive1)
    place_both(g_qkv, WIDTH, own[0], other[0])
    place_both(g_qkv, WIDTH + 384, own[1][:, :128], other[1][:, :128])
    place_both(g_qkv, 2 * WIDTH, own[1][:, 128:], other[1][:, 128:])
    place_both(g_qkv, 2 * WIDTH + 256, own[2], other[2])
    for copy in sent:
        copy.wait_send()


def hand_over(*refs):
    for source, target in zip(refs[:4], refs[4:]):
        target[...] = source[...]


def on_device(latent, predictions, target, area_weight, slab_count, w_qkv, w_o, w_out):
    members_here, points, width = latent.shape
    channels = predictions.shape[1]
    rows = members_here * points
    vmem = pl.BlockSpec(memory_space=pltpu.VMEM)
    hbm = pl.BlockSpec(memory_space=pl.ANY)
    smem = pl.BlockSpec(memory_space=pltpu.SMEM)
    shapes = (
        jax.ShapeDtypeStruct((rows, width), BF16),
        jax.ShapeDtypeStruct((8, 3 * width), F32),
        jax.ShapeDtypeStruct((8, width), F32),
        jax.ShapeDtypeStruct((8, channels), F32),
    )
    grad_latent, grad_qkv, grad_o, grad_out = pl.pallas_call(
        kernel,
        out_shape=shapes,
        in_specs=[hbm, vmem, vmem, vmem, smem, hbm, hbm, vmem],
        out_specs=[vmem] * 4,
        scratch_shapes=SHAPES,
        compiler_params=pltpu.CompilerParams(
            collective_id=0, has_side_effects=True, vmem_limit_bytes=62 * 1024 * 1024
        ),
    )(
        latent.reshape(rows, width), predictions.transpose(1, 0, 2), target, area_weight.reshape(1, points),
        slab_count, w_qkv, w_o, w_out.T,
    )
    grad_latent, grad_qkv, grad_o, grad_out = pl.pallas_call(
        hand_over,
        out_shape=shapes,
        in_specs=[vmem] * 4,
        out_specs=[vmem] * 4,
    )(grad_latent, grad_qkv, grad_o, grad_out)
    return grad_latent.reshape(latent.shape), grad_qkv, grad_o, grad_out


def solution(mesh):
    placed = (
        P("member", "space", None),
        P("member", None, "space"),
        P(None, "space"),
        P("space"),
        P("space"),
        P(),
        P(),
        P(),
    )
    return jax.shard_map(
        on_device,
        mesh=mesh,
        in_specs=placed,
        out_specs=(
            P("member", "space", None),
            P(("member", "space"), None),
            P(("member", "space"), None),
            P(("member", "space"), None),
        ),
        check_vma=False,
    )
```

```python
from types import SimpleNamespace

import jax
import jax.numpy as jnp
from jax import lax
from jax.experimental import pallas as pl
from jax.experimental.pallas import tpu as pltpu
from jax.sharding import PartitionSpec as P

RING = 4
MEMBERS_DEV = 2
ROWS = 256
WIDTH = 1024
HALF = 512
GROUP = 256
CHANNEL_GROUP = 16
LOG2E = 1.4426950408889634
F32 = jnp.float32
BF16 = jnp.bfloat16
MESH = pl.DeviceIdType.MESH

ORDERS = (("x", "y", "z"), ("y", "z", "x"), ("z", "x", "y"))
WIDTHS = ((384, 384, 384), (384, 384, 256))


class Place:
    def __init__(self):
        self.member = lax.axis_index("member")
        self.space = lax.axis_index("space")
        self.core = self.space % 2
        z_lo = (self.space // 2) % 2
        z_hi = self.member % 2
        self.at = {"x": self.space // 4, "y": self.member // 2, "z": z_hi * 2 + z_lo}

    def partner(self, axis, index):
        if axis == "x":
            return (self.member, index * 4 + self.space % 4)
        if axis == "y":
            return (index * 2 + self.member % 2, self.space)
        member = (self.member // 2) * 2 + index // 2
        return (member, (self.space // 4) * 4 + (index % 2) * 2 + self.core)

    def pair(self):
        return (self.member, self.space + 1 - 2 * self.core)

    def right(self):
        return (self.member, (self.space + 1) % 16)

    def left(self):
        return (self.member, (self.space + 15) % 16)

    def across(self, axis, offset):
        member, space = self.partner(axis, self.ahead(axis, offset))
        return (member, space + 1 - 2 * self.core)

    def ahead(self, axis, offset):
        return (self.at[axis] + offset) % RING


def chunk_order(order):
    where = []
    for y in range(4):
        for z_hi in range(2):
            for x in range(4):
                for z_lo in range(2):
                    digit = {"x": x, "y": y, "z": z_hi * 2 + z_lo}
                    a, b, c = (digit[name] for name in order)
                    where.append(a * 16 + b * 4 + c)
    return where


def remote(src, dst, send, recv, device):
    return pltpu.make_async_remote_copy(
        src_ref=src, dst_ref=dst, send_sem=send, recv_sem=recv, device_id=device, device_id_type=MESH
    )


def dot(a, b):
    return jnp.dot(a, b, preferred_element_type=F32)


def dot_nt(a, b):
    return lax.dot_general(a, b, (((1,), (1,)), ((), ())), preferred_element_type=F32)


def sign_of(a, b):
    one = jnp.float32(1.0)
    zero = jnp.float32(0.0)
    return jnp.where(a > b, one, zero) - jnp.where(a < b, one, zero)


def scratch():
    vmem = pltpu.VMEM
    dma = pltpu.SemaphoreType.DMA
    block3 = vmem((3, ROWS, WIDTH), BF16)
    rows_b = vmem((ROWS, WIDTH), BF16)
    rows_f = vmem((ROWS, WIDTH), F32)
    factor = vmem((2 * ROWS, HALF), BF16)
    turned = vmem((WIDTH, 2 * ROWS), BF16)

    def waves(*shape, dtype):
        return [[vmem((*shape, w), dtype) for w in widths] for widths in WIDTHS]

    return dict(
        w_in=vmem((WIDTH, 3 * WIDTH), BF16),
        w_back=vmem((WIDTH, WIDTH), BF16),
        w_dec=vmem((128, WIDTH), BF16),
        lat=block3, xn=block3, qx=block3, kx=block3, vx=block3, dx=block3,
        norm=rows_f, daf=rows_f, dk_acc=rows_f, dv_acc=rows_f, dnorm=rows_f,
        rstd=vmem((ROWS, 128), F32),
        daf_b=block3,
        att=rows_b, att_o=rows_b,
        dqkv=vmem((ROWS, 3 * WIDTH), BF16),
        mask=vmem((4 * 128, GROUP), BF16),
        stat=vmem((2, 2, 8, 512), F32),
        stat_n=vmem((2, 2, 2, 8, 512), F32),
        pred_p=vmem((2, 128, 128), F32),
        targ_p=vmem((128, 128), F32),
        pred_g=vmem((8, 2, CHANNEL_GROUP, 128), F32),
        crps_g=vmem((8, 2, CHANNEL_GROUP, 128), BF16),
        cr=vmem((3, 2, 128, 128), BF16),
        cr_rows=vmem((ROWS, 128), BF16),
        d_q=factor, d_k=factor, d_v=factor, d_o=factor,
        xt=[turned] * 3,
        at=[turned] * 2,
        ft=vmem((WIDTH, ROWS), BF16),
        send1=waves(6, 128, dtype=BF16),
        recv1=waves(6, 128, dtype=BF16),
        hold=waves(2, 128, dtype=F32),
        acc1=waves(256, dtype=F32),
        send2=waves(3, 64, dtype=BF16),
        recv2=waves(3, 64, dtype=BF16),
        acc2=waves(64, dtype=F32),
        recv3=waves(7, 8, dtype=F32),
        load=dma((5,)),
        halo_s=dma((3,)), halo_r=dma((3,)),
        pred_s=dma((7,)), pred_r=dma((7,)),
        back_s=dma((7,)), back_r=dma((7,)),
        crh_s=dma((2,)), crh_r=dma((2,)),
        sth_s=dma((4,)), sth_r=dma((4,)),
        pair_s=dma((6,)), pair_r=dma((6,)),
        ring_s=dma((96,)), ring_r=dma((96,)),
    )


SHAPES, TREE = jax.tree.flatten(scratch())


def kernel(
    latent, predictions, target, area_weight, slab_count, w_qkv, w_o, w_out, g_latent, g_qkv, g_o, g_out, *buffers
):
    r = SimpleNamespace(**jax.tree.unflatten(TREE, buffers))
    place = Place()
    core, member, slab = place.core, place.member, place.space
    sent = []

    def start(copy):
        copy.start()
        sent.append(copy)
        return copy

    load = r.load
    loads = [
        pltpu.make_async_copy(latent, r.lat.at[1], load.at[0]),
        pltpu.make_async_copy(w_qkv.at[:, pl.ds(0, WIDTH)], r.w_in.at[:, pl.ds(0, WIDTH)], load.at[1]),
        pltpu.make_async_copy(w_qkv.at[:, pl.ds(WIDTH, WIDTH)], r.w_in.at[:, pl.ds(WIDTH, WIDTH)], load.at[2]),
        pltpu.make_async_copy(
            w_qkv.at[:, pl.ds(2 * WIDTH, WIDTH)], r.w_in.at[:, pl.ds(2 * WIDTH, WIDTH)], load.at[3]
        ),
        pltpu.make_async_copy(w_o, r.w_back, load.at[4]),
    ]
    for copy in loads:
        copy.start()

    barrier = pltpu.get_barrier_semaphore()
    greeted = [((member + o) % 8, slab) for o in range(1, 8)]
    greeted += [place.partner(axis, place.ahead(axis, o)) for axis in ("x", "z") for o in (1, 2, 3)]
    greeted += [place.right(), place.left()]
    greeted += [place.across(axis, o) for axis in ("x", "y", "z") for o in (1, 2, 3)]
    for device in greeted:
        pl.semaphore_signal(barrier, inc=1, device_id=device, device_id_type=MESH)

    r.pred_p[:, 96:, :] = jnp.zeros((2, 32, 128), F32)
    channels = target.shape[0]
    for m in range(MEMBERS_DEV):
        r.pred_p[m, :channels, :] = predictions[:, m, :]

    pl.semaphore_wait(barrier, len(greeted))

    pred_copies = []
    for o in range(1, 8):
        dest = (member + o) % 8
        pred_copies.append(start(remote(
            r.pred_p.at[:, pl.ds(pl.multiple_of(dest * CHANNEL_GROUP, CHANNEL_GROUP), CHANNEL_GROUP)],
            r.pred_g.at[member], r.pred_s.at[o - 1], r.pred_r.at[o - 1], (dest, slab),
        )))
    near, far = 2 - 2 * core, 2 * core
    far_device = (member, (slab + 15 + 2 * core) % 16)
    halo_near = start(remote(latent, r.lat.at[far], r.halo_s.at[0], r.halo_r.at[0], place.pair()))

    def halo_part(i):
        rows = pl.ds(i * 128, 128)
        return start(remote(
            latent.at[rows], r.lat.at[near, rows], r.halo_s.at[1 + i], r.halo_r.at[1 + i], far_device
        ))

    halo_far = [halo_part(0)]

    r.targ_p[...] = jnp.zeros((128, 128), F32)
    r.w_dec[...] = jnp.zeros((128, WIDTH), BF16)
    r.targ_p[:channels, :] = target[...]
    r.w_dec[:channels, :] = w_out[...]
    head_row = lax.broadcasted_iota(jnp.int32, (512, GROUP), 0) // 128
    head_col = lax.broadcasted_iota(jnp.int32, (512, GROUP), 1) // 64
    r.mask[...] = jnp.where(head_row == head_col, jnp.float32(1.0), jnp.float32(0.0)).astype(BF16)

    every = slice(0, ROWS)

    def normalise(block, keep, rows=every):
        xf = r.lat[block, rows, :].astype(F32)
        mean = jnp.mean(xf, axis=-1, keepdims=True)
        cent = xf - mean
        var = jnp.mean(cent * cent, axis=-1, keepdims=True)
        rstd = lax.rsqrt(var + 1e-05)
        norm = cent * rstd
        r.xn[block, rows, :] = norm.astype(BF16)
        if keep:
            r.norm[...] = norm
            r.rstd[...] = jnp.broadcast_to(rstd, (ROWS, 128))

    def project(block, begin, end, rows=every):
        for j in range(begin, end):
            piece = dot(r.xn[block, rows, :], r.w_in[:, j * HALF : (j + 1) * HALF]).astype(BF16)
            at = slice((j % 2) * HALF, (j % 2 + 1) * HALF)
            if j < 2:
                r.qx[block, rows, at] = piece * jnp.bfloat16(0.125)
            elif j < 4:
                r.kx[block, rows, at] = piece
            else:
                r.vx[block, rows, at] = piece

    loads[0].wait()
    normalise(1, True)
    for copy in loads[1:]:
        copy.wait()
    project(1, 0, 6)

    r.pred_g[member] = r.pred_p[:, pl.ds(pl.multiple_of(member * CHANNEL_GROUP, CHANNEL_GROUP), CHANNEL_GROUP), :]
    for copy in pred_copies:
        copy.wait_recv()
    y = [r.pred_g[i // 2, i % 2] for i in range(16)]
    pair_sum = [jnp.zeros((CHANNEL_GROUP, 128), F32) for _ in range(16)]
    for i in range(16):
        for k in range(i + 1, 16):
            s = sign_of(y[i], y[k])
            pair_sum[i] = pair_sum[i] + s
            pair_sum[k] = pair_sum[k] - s
    point = lax.broadcasted_iota(jnp.int32, (1, 128), 1)
    pweight = jnp.where(point < slab_count[0], area_weight[...], jnp.zeros((1, 128), F32))
    truth = r.targ_p[pl.ds(pl.multiple_of(member * CHANNEL_GROUP, CHANNEL_GROUP), CHANNEL_GROUP), :]
    for i in range(16):
        crps = pweight * (sign_of(y[i], truth) - pair_sum[i] / 15.0)
        r.crps_g[i // 2, i % 2] = crps.astype(BF16)
    own_group = pl.ds(pl.multiple_of(member * CHANNEL_GROUP, CHANNEL_GROUP), CHANNEL_GROUP)
    back_copies = []
    for o in range(1, 8):
        dest = (member + o) % 8
        back_copies.append(start(remote(
            r.crps_g.at[dest], r.cr.at[1, :, own_group], r.back_s.at[o - 1], r.back_r.at[o - 1], (dest, slab)
        )))
    r.cr[1, :, own_group, :] = r.crps_g[member]

    halo_far.append(halo_part(1))

    def decode(block):
        for m in range(2):
            turned = r.cr[block, m].T
            value = dot(turned, r.w_dec[...])
            at = slice(m * 128, m * 128 + 128)
            r.daf_b[block, at, :] = value.astype(BF16)
            if isinstance(block, int):
                r.daf[at, :] = value
                r.cr_rows[at, :] = turned

    def attend_back(block):
        for j in range(4):
            at = slice(j * GROUP, (j + 1) * GROUP)
            r.dx[block, :, at] = dot_nt(r.daf_b[block], r.w_back[at, :]).astype(BF16)

    def lay(value, targets, column):
        turned = value.T
        for ref, order in targets:
            for chunk, spot in enumerate(chunk_order(order)):
                ref[spot * 16 : spot * 16 + 16, column : column + ROWS] = turned[chunk * 16 : chunk * 16 + 16]

    xts = [(r.xt[0], ORDERS[0]), (r.xt[1], ORDERS[1]), (r.xt[2], ORDERS[2])]
    ats = [(r.at[0], ORDERS[1]), (r.at[1], ORDERS[2])]
    theirs = pl.multiple_of((1 - core) * HALF, HALF)
    high_rows = pl.ds(ROWS, ROWS)

    def give(i, src, dst):
        return start(remote(src, dst, r.pair_s.at[i], r.pair_r.at[i], place.pair()))

    halo_near.wait_recv()
    normalise(near, False)
    project(near, 0, 6)
    lay(r.xn[1], xts, 0)
    lay(r.xn[near], xts, ROWS)
    halo_far[0].wait_recv()
    member_rows = [slice(0, 128), slice(128, 256)]
    normalise(far, False, member_rows[0])
    project(far, 2, 6, member_rows[0])
    for copy in back_copies:
        copy.wait_recv()
    crh_near = start(remote(r.cr.at[1], r.cr.at[far], r.crh_s.at[0], r.crh_r.at[0], place.pair()))
    crh_far = start(remote(r.cr.at[1], r.cr.at[near], r.crh_s.at[1], r.crh_r.at[1], far_device))
    decode(1)
    pair_o = give(0, r.daf_b.at[1, :, pl.ds(theirs, HALF)], r.d_o.at[high_rows])
    attend_back(1)

    edge = [
        jnp.where(slab > 0, jnp.float32(0.0), jnp.float32(-1e30)),
        jnp.where(slab < 15, jnp.float32(0.0), jnp.float32(-1e30)),
    ]

    def spread(block):
        return jnp.concatenate([block, block, block, block], axis=0) * r.mask[...]

    def per_head(left, right):
        return jnp.concatenate(
            [dot(left[h * 64 : (h + 1) * 64], right[:, h * 128 : (h + 1) * 128]) for h in range(4)], axis=0
        ).T

    def group_cols(half, u, begin=0):
        return pl.ds(pl.multiple_of(begin + half * HALF + u * GROUP, GROUP), GROUP)

    def own_queries(m, half):
        rows = member_rows[m]
        for u in range(2):
            cols = group_cols(half, u)
            keys = jnp.concatenate([r.kx[b, rows, cols] for b in range(3)], axis=0)
            values = jnp.concatenate([r.vx[b, rows, cols] for b in range(3)], axis=0)
            q_b = spread(r.qx[1, rows, cols])
            d_b = spread(r.dx[1, rows, cols])
            scores = dot_nt(keys, q_b)
            scores = jnp.concatenate([scores[:128] + edge[0], scores[128:256], scores[256:] + edge[1]], axis=0)
            top = jnp.max(scores, axis=0, keepdims=True) * LOG2E
            e = jnp.exp2(scores * LOG2E - top)
            total = jnp.sum(e, axis=0, keepdims=True)
            prob = e * (1.0 / total)
            prob_b = prob.astype(BF16)
            dprob = dot_nt(values, d_b)
            delta = jnp.sum(dprob * prob, axis=0, keepdims=True)
            dscore = (prob * (dprob - delta)).astype(BF16)
            r.att[rows, cols] = per_head(values.T, prob_b).astype(BF16)
            r.dqkv[rows, cols] = (per_head(keys.T, dscore) * 0.125).astype(BF16)
            r.dk_acc[rows, cols] = dot(dscore[128:256], q_b)
            r.dv_acc[rows, cols] = dot(prob_b[128:256], d_b)
            r.stat[m, half, 2 * u : 2 * u + 1, :] = top + jnp.log2(total)
            r.stat[m, half, 2 * u + 1 : 2 * u + 2, :] = delta

    def send_stat(m):
        return [
            start(remote(
                r.stat.at[m], r.stat_n.at[core, m], r.sth_s.at[2 * m], r.sth_r.at[2 * m], place.pair()
            )),
            start(remote(
                r.stat.at[m], r.stat_n.at[1 - core, m], r.sth_s.at[2 * m + 1], r.sth_r.at[2 * m + 1], far_device
            )),
        ]

    r.stat[...] = jnp.zeros((2, 2, 8, 512), F32)
    own_queries(0, 1 - core)
    own_queries(0, core)
    sth = send_stat(0)
    halo_far[1].wait_recv()
    normalise(far, False, member_rows[1])
    project(far, 2, 6, member_rows[1])
    own_queries(1, 1 - core)
    own_half = pl.multiple_of(core * HALF, HALF)
    pair_q = give(1, r.dqkv.at[:, pl.ds(theirs, HALF)], r.d_q.at[high_rows])
    pair_a = [give(2, r.att.at[:, pl.ds(theirs, HALF)], r.att_o.at[:, pl.ds(theirs, HALF)])]
    own_queries(1, core)
    sth += send_stat(1)
    pair_a.append(give(3, r.att.at[:, pl.ds(own_half, HALF)], r.att_o.at[:, pl.ds(own_half, HALF)]))

    def mine(ref, at, begin):
        return jnp.where(core == 0, ref[at, begin : begin + HALF], ref[at, begin + HALF : begin + 2 * HALF])

    r.d_o[:ROWS] = mine(r.daf_b.at[1], slice(0, ROWS), 0)
    r.d_q[:ROWS] = mine(r.dqkv, slice(0, ROWS), 0)

    after = r.lat[1].astype(F32) + dot(r.att[...], r.w_back[...])
    lay(after.astype(BF16), [(r.ft, ORDERS[2])], 0)
    lay(r.att[...], ats, 0)
    for copy in pair_a:
        copy.wait_recv()
    lay(r.att_o[...], ats, ROWS)

    def terms(wave, p, dest):
        at = pl.ds(pl.multiple_of(dest * 256, 256), 256)
        if wave == 0:
            if p == 0:
                return [dot(r.xt[0][at, :], r.d_q[:, :384])]
            if p == 1:
                return [dot(r.xt[1][at, :], r.d_q[:, 384:]), dot(r.at[0][at, :], r.d_o[:, :256])]
            return [dot(r.at[1][at, :], r.d_o[:, 256:]), dot(r.ft[at, :], r.cr_rows[...])]
        if p == 0:
            return [dot(r.xt[0][at, :], r.d_k[:, :384])]
        if p == 1:
            return [dot(r.xt[1][at, :], r.d_k[:, 384:]), dot(r.xt[1][at, :], r.d_v[:, :256])]
        return [dot(r.xt[2][at, :], r.d_v[:, 256:])]

    def push(wave, p, slot, src, dst, device):
        slot = (wave * 3 + p) * 16 + slot
        return start(remote(src, dst, r.ring_s.at[slot], r.ring_r.at[slot], device))

    def neighbour(p, phase, offset):
        axis = ORDERS[p][phase]
        return place.partner(axis, place.ahead(axis, offset))

    def put(ref, index, values, dtype, rows=slice(None)):
        begin = 0
        for value in values:
            end = begin + value.shape[1]
            ref[index, rows, begin:end] = value.astype(dtype)
            begin = end

    def first(wave):
        copies = {}

        def go(p, slot, offset):
            copies[p, slot] = push(
                wave, p, slot, r.send1[wave][p].at[slot], r.recv1[wave][p].at[slot], neighbour(p, 0, offset)
            )

        for p in range(3):
            values = terms(wave, p, place.ahead(ORDERS[p][0], 2))
            put(r.send1[wave][p], 0, [v[:128] for v in values], BF16)
            put(r.send1[wave][p], 1, [v[128:] for v in values], BF16)
            go(p, 0, 1)
            go(p, 1, 3)
        for p in range(3):
            values = terms(wave, p, place.ahead(ORDERS[p][0], 1))
            put(r.send1[wave][p], 2, [v[128:] for v in values], BF16)
            put(r.hold[wave][p], 0, [v[:128] for v in values], F32)
            go(p, 2, 1)
            values = terms(wave, p, place.ahead(ORDERS[p][0], 3))
            put(r.send1[wave][p], 3, [v[:128] for v in values], BF16)
            put(r.hold[wave][p], 1, [v[128:] for v in values], F32)
            go(p, 3, 3)
        return copies

    def relay(wave, copies):
        for p in range(3):
            for half, offset in ((0, 1), (1, 3)):
                copies[p, half].wait_recv()
                r.send1[wave][p][4 + half] = (r.hold[wave][p][half] + r.recv1[wave][p][half].astype(F32)).astype(BF16)
                copies[p, 4 + half] = push(
                    wave, p, 4 + half, r.send1[wave][p].at[4 + half], r.recv1[wave][p].at[4 + half],
                    neighbour(p, 0, offset),
                )

    def own_terms(wave):
        for p in range(3):
            begin = 0
            for value in terms(wave, p, place.at[ORDERS[p][0]]):
                end = begin + value.shape[1]
                r.acc1[wave][p][:, begin:end] = value
                begin = end

    def second(wave, arrivals):
        copies = {}
        for p in range(3):
            acc, came = r.acc1[wave][p], r.recv1[wave][p]
            for slot in (2, 3, 4, 5):
                arrivals[p, slot].wait_recv()
            acc[:128] += came[3].astype(F32) + came[4].astype(F32)
            acc[128:] += came[2].astype(F32) + came[5].astype(F32)
            for offset in (2, 1, 3):
                dest = place.ahead(ORDERS[p][1], offset)
                r.send2[wave][p][offset - 1] = acc[pl.ds(pl.multiple_of(dest * 64, 64), 64), :].astype(BF16)
                copies[p, offset] = push(
                    wave, p, 5 + offset, r.send2[wave][p].at[offset - 1], r.recv2[wave][p].at[offset - 1],
                    neighbour(p, 1, offset),
                )
        return copies

    def third(wave, arrivals):
        copies = []
        for p in range(3):
            for offset in (1, 2, 3):
                arrivals[p, offset].wait_recv()
            own = r.acc1[wave][p][pl.ds(pl.multiple_of(place.at[ORDERS[p][1]] * 64, 64), 64), :]
            came = r.recv2[wave][p]
            r.acc2[wave][p][...] = own + (came[0].astype(F32) + came[1].astype(F32) + came[2].astype(F32))
            for offset in (2, 1, 3, 0):
                dest = place.ahead(ORDERS[p][2], offset)
                device = neighbour(p, 2, offset)
                for other in ((0, 1) if offset else (1,)):
                    side = core if other == 0 else 1 - core
                    slot = 3 + offset if other else offset - 1
                    src = r.acc2[wave][p].at[pl.ds(pl.multiple_of(dest * 16 + side * 8, 8), 8)]
                    to = (device[0], device[1] + (side - core))
                    copies.append(push(wave, p, 9 + slot, src, r.recv3[wave][p].at[slot], to))
        return copies

    def finish(wave, arrivals):
        for copy in arrivals:
            copy.wait_recv()
        own, other = [], []
        for p in range(3):
            came = r.recv3[wave][p]
            at = pl.ds(pl.multiple_of(place.at[ORDERS[p][2]] * 16 + core * 8, 8), 8)
            own.append(r.acc2[wave][p][at, :] + came[0] + came[1] + came[2])
            other.append(came[3] + came[4] + came[5] + came[6])
        return own, other

    def place_both(out, begin, own, other):
        width = own.shape[1]
        out[:, begin : begin + width] = jnp.where(core == 0, own, other)
        out[:, begin + HALF : begin + HALF + width] = jnp.where(core == 0, other, own)

    pair_o.wait_recv()
    pair_q.wait_recv()
    arrive0 = first(0)
    own_terms(0)

    for side, copy in ((near, crh_near), (far, crh_far)):
        copy.wait_recv()
        decode(side)
        attend_back(side)
    project(far, 0, 2)

    def other_queries(half):
        for m in range(2):
            rows = member_rows[m]
            for u in range(2):
                cols = group_cols(half, u)
                keys = r.kx[1, rows, cols]
                values = r.vx[1, rows, cols]
                dk = r.dk_acc[rows, cols]
                dv = r.dv_acc[rows, cols]
                for side in range(2):
                    q_b = spread(r.qx[2 * side, rows, cols])
                    d_b = spread(r.dx[2 * side, rows, cols])
                    lse = r.stat_n[side, m, half, 2 * u : 2 * u + 1, :]
                    delta = r.stat_n[side, m, half, 2 * u + 1 : 2 * u + 2, :]
                    prob = jnp.exp2(dot_nt(keys, q_b) * LOG2E - (lse - edge[side]))
                    dscore = (prob * (dot_nt(values, d_b) - delta)).astype(BF16)
                    dk += dot(dscore, q_b)
                    dv += dot(prob.astype(BF16), d_b)
                r.dqkv[rows, group_cols(half, u, WIDTH)] = dk.astype(BF16)
                r.dqkv[rows, group_cols(half, u, 2 * WIDTH)] = dv.astype(BF16)

    for copy in sth:
        copy.wait_recv()
    other_queries(1 - core)
    pair_k = give(4, r.dqkv.at[:, pl.ds(pl.multiple_of(WIDTH + theirs, HALF), HALF)], r.d_k.at[high_rows])
    pair_v = give(5, r.dqkv.at[:, pl.ds(pl.multiple_of(2 * WIDTH + theirs, HALF), HALF)], r.d_v.at[high_rows])
    relay(0, arrive0)
    other_queries(core)
    r.d_k[:ROWS] = mine(r.dqkv, slice(0, ROWS), WIDTH)
    r.d_v[:ROWS] = mine(r.dqkv, slice(0, ROWS), 2 * WIDTH)
    pair_k.wait_recv()
    pair_v.wait_recv()
    arrive1 = first(1)
    arrive0 = second(0, arrive0)
    own_terms(1)

    for j in range(4):
        at = slice(j * GROUP, (j + 1) * GROUP)
        r.dnorm[:, at] = dot_nt(r.dqkv[...], r.w_in[at, :])
    relay(1, arrive1)
    arrive0 = third(0, arrive0)
    dnorm = r.dnorm[...]
    norm = r.norm[...]
    dlayer = r.rstd[:, :1] * (
        dnorm
        - jnp.mean(dnorm, axis=-1, keepdims=True)
        - norm * jnp.mean(dnorm * norm, axis=-1, keepdims=True)
    )
    g_latent[...] = (r.daf[...] + dlayer).astype(BF16)

    arrive1 = second(1, arrive1)
    own, other = finish(0, arrive0)
    place_both(g_qkv, 0, own[0], other[0])
    place_both(g_qkv, 384, own[1][:, :128], other[1][:, :128])
    place_both(g_o, 0, own[1][:, 128:], other[1][:, 128:])
    place_both(g_o, 256, own[2][:, :256], other[2][:, :256])
    total = own[2][:, 256:] + other[2][:, 256:]
    g_out[...] = total[:, :channels]

    arrive1 = third(1, arrive1)
    own, other = finish(1, arrive1)
    place_both(g_qkv, WIDTH, own[0], other[0])
    place_both(g_qkv, WIDTH + 384, own[1][:, :128], other[1][:, :128])
    place_both(g_qkv, 2 * WIDTH, own[1][:, 128:], other[1][:, 128:])
    place_both(g_qkv, 2 * WIDTH + 256, own[2], other[2])
    for copy in sent:
        copy.wait_send()


def hand_over(*refs):
    for source, target in zip(refs[:4], refs[4:]):
        target[...] = source[...]


def on_device(latent, predictions, target, area_weight, slab_count, w_qkv, w_o, w_out):
    members_here, points, width = latent.shape
    channels = predictions.shape[1]
    rows = members_here * points
    vmem = pl.BlockSpec(memory_space=pltpu.VMEM)
    hbm = pl.BlockSpec(memory_space=pl.ANY)
    smem = pl.BlockSpec(memory_space=pltpu.SMEM)
    shapes = (
        jax.ShapeDtypeStruct((rows, width), BF16),
        jax.ShapeDtypeStruct((8, 3 * width), F32),
        jax.ShapeDtypeStruct((8, width), F32),
        jax.ShapeDtypeStruct((8, channels), F32),
    )
    grad_latent, grad_qkv, grad_o, grad_out = pl.pallas_call(
        kernel,
        out_shape=shapes,
        in_specs=[hbm, vmem, vmem, vmem, smem, hbm, hbm, vmem],
        out_specs=[vmem] * 4,
        scratch_shapes=SHAPES,
        compiler_params=pltpu.CompilerParams(
            collective_id=0, has_side_effects=True, vmem_limit_bytes=62 * 1024 * 1024
        ),
    )(
        latent.reshape(rows, width), predictions.transpose(1, 0, 2), target, area_weight.reshape(1, points),
        slab_count, w_qkv, w_o, w_out.T,
    )
    grad_latent, grad_qkv, grad_o, grad_out = pl.pallas_call(
        hand_over,
        out_shape=shapes,
        in_specs=[vmem] * 4,
        out_specs=[vmem] * 4,
    )(grad_latent, grad_qkv, grad_o, grad_out)
    return grad_latent.reshape(latent.shape), grad_qkv, grad_o, grad_out


def solution(mesh):
    placed = (
        P("member", "space", None),
        P("member", None, "space"),
        P(None, "space"),
        P("space"),
        P("space"),
        P(),
        P(),
        P(),
    )
    return jax.shard_map(
        on_device,
        mesh=mesh,
        in_specs=placed,
        out_specs=(
            P("member", "space", None),
            P(("member", "space"), None),
            P(("member", "space"), None),
            P(("member", "space"), None),
        ),
        check_vma=False,
    )
```

```python
from types import SimpleNamespace

import jax
import jax.numpy as jnp
from jax import lax
from jax.experimental import pallas as pl
from jax.experimental.pallas import tpu as pltpu
from jax.sharding import PartitionSpec as P

RING = 4
MEMBERS_DEV = 2
ROWS = 256
WIDTH = 1024
HALF = 512
GROUP = 256
CHANNEL_GROUP = 16
LOG2E = 1.4426950408889634
F32 = jnp.float32
BF16 = jnp.bfloat16
MESH = pl.DeviceIdType.MESH

ORDERS = (("x", "y", "z"), ("y", "z", "x"), ("z", "x", "y"))
WIDTHS = ((384, 384, 384), (384, 384, 256))


class Place:
    def __init__(self):
        self.member = lax.axis_index("member")
        self.space = lax.axis_index("space")
        self.core = self.space % 2
        z_lo = (self.space // 2) % 2
        z_hi = self.member % 2
        self.at = {"x": self.space // 4, "y": self.member // 2, "z": z_hi * 2 + z_lo}

    def partner(self, axis, index):
        if axis == "x":
            return (self.member, index * 4 + self.space % 4)
        if axis == "y":
            return (index * 2 + self.member % 2, self.space)
        member = (self.member // 2) * 2 + index // 2
        return (member, (self.space // 4) * 4 + (index % 2) * 2 + self.core)

    def pair(self):
        return (self.member, self.space + 1 - 2 * self.core)

    def right(self):
        return (self.member, (self.space + 1) % 16)

    def left(self):
        return (self.member, (self.space + 15) % 16)

    def across(self, axis, offset):
        member, space = self.partner(axis, self.ahead(axis, offset))
        return (member, space + 1 - 2 * self.core)

    def ahead(self, axis, offset):
        return (self.at[axis] + offset) % RING


def chunk_order(order):
    where = []
    for y in range(4):
        for z_hi in range(2):
            for x in range(4):
                for z_lo in range(2):
                    digit = {"x": x, "y": y, "z": z_hi * 2 + z_lo}
                    a, b, c = (digit[name] for name in order)
                    where.append(a * 16 + b * 4 + c)
    return where


def remote(src, dst, send, recv, device):
    return pltpu.make_async_remote_copy(
        src_ref=src, dst_ref=dst, send_sem=send, recv_sem=recv, device_id=device, device_id_type=MESH
    )


def dot(a, b):
    return jnp.dot(a, b, preferred_element_type=F32)


def dot_nt(a, b):
    return lax.dot_general(a, b, (((1,), (1,)), ((), ())), preferred_element_type=F32)


def sign_of(a, b):
    one = jnp.float32(1.0)
    zero = jnp.float32(0.0)
    return jnp.where(a > b, one, zero) - jnp.where(a < b, one, zero)


def scratch():
    vmem = pltpu.VMEM
    dma = pltpu.SemaphoreType.DMA
    block3 = vmem((3, ROWS, WIDTH), BF16)
    rows_b = vmem((ROWS, WIDTH), BF16)
    rows_f = vmem((ROWS, WIDTH), F32)
    factor = vmem((2 * ROWS, HALF), BF16)
    turned = vmem((WIDTH, 2 * ROWS), BF16)

    def waves(*shape, dtype):
        return [[vmem((*shape, w), dtype) for w in widths] for widths in WIDTHS]

    return dict(
        w_in=vmem((WIDTH, 3 * WIDTH), BF16),
        w_back=vmem((WIDTH, WIDTH), BF16),
        w_dec=vmem((128, WIDTH), BF16),
        lat=block3, xn=block3, qx=block3, kx=block3, vx=block3, dx=block3,
        norm=rows_f, daf=rows_f, dk_acc=rows_f, dv_acc=rows_f, dnorm=rows_f,
        rstd=vmem((ROWS, 128), F32),
        daf_b=block3,
        att=rows_b, att_o=rows_b,
        dqkv=vmem((ROWS, 3 * WIDTH), BF16),
        mask=vmem((2, 128, 128), BF16),
        pred_in=vmem((200, 128), F32),
        targ_in=vmem((100, 128), F32),
        w_out_in=vmem((100, WIDTH), BF16),
        g_stage=vmem((ROWS, WIDTH), BF16),
        stat=vmem((2, 2, 8, 512), F32),
        stat_n=vmem((2, 2, 2, 8, 512), F32),
        pred_p=vmem((2, 128, 128), F32),
        targ_p=vmem((128, 128), F32),
        pred_g=vmem((8, 2, CHANNEL_GROUP, 128), F32),
        crps_g=vmem((8, 2, CHANNEL_GROUP, 128), BF16),
        cr=vmem((3, 2, 128, 128), BF16),
        cr_rows=vmem((ROWS, 128), BF16),
        d_q=factor, d_k=factor, d_v=factor, d_o=factor,
        xt=[turned] * 3,
        at=[turned] * 2,
        ft=vmem((WIDTH, ROWS), BF16),
        send1=waves(6, 128, dtype=BF16),
        recv1=waves(6, 128, dtype=BF16),
        hold=waves(2, 128, dtype=F32),
        acc1=waves(256, dtype=F32),
        send2=waves(3, 64, dtype=BF16),
        recv2=waves(3, 64, dtype=BF16),
        acc2=waves(64, dtype=F32),
        recv3=waves(7, 8, dtype=F32),
        load=dma((9,)),
        halo_s=dma((3,)), halo_r=dma((3,)),
        pred_s=dma((7,)), pred_r=dma((7,)),
        back_s=dma((7,)), back_r=dma((7,)),
        crh_s=dma((2,)), crh_r=dma((2,)),
        sth_s=dma((4,)), sth_r=dma((4,)),
        pair_s=dma((6,)), pair_r=dma((6,)),
        ring_s=dma((96,)), ring_r=dma((96,)),
    )


SHAPES, TREE = jax.tree.flatten(scratch())


def kernel(
    latent, predictions, target, area_weight, slab_count, w_qkv, w_o, w_out, g_latent, g_qkv, g_o, g_out, *buffers
):
    r = SimpleNamespace(**jax.tree.unflatten(TREE, buffers))
    place = Place()
    core, member, slab = place.core, place.member, place.space
    sent = []

    def start(copy):
        copy.start()
        sent.append(copy)
        return copy

    load = r.load
    moves = [(predictions, r.pred_in), (latent, r.lat.at[1]), (target, r.targ_in), (w_out, r.w_out_in)]
    for j in range(3):
        third_cols = pl.ds(j * WIDTH, WIDTH)
        moves.append((w_qkv.at[:, third_cols], r.w_in.at[:, third_cols]))
    moves.append((w_o, r.w_back))
    loads = [pltpu.make_async_copy(src, dst, load.at[i]) for i, (src, dst) in enumerate(moves)]
    for copy in loads:
        copy.start()

    barrier = pltpu.get_barrier_semaphore()
    greeted = [((member + o) % 8, slab) for o in range(1, 8)]
    greeted += [place.partner(axis, place.ahead(axis, o)) for axis in ("x", "z") for o in (1, 2, 3)]
    greeted += [place.right(), place.left()]
    greeted += [place.across(axis, o) for axis in ("x", "y", "z") for o in (1, 2, 3)]
    for device in greeted:
        pl.semaphore_signal(barrier, inc=1, device_id=device, device_id_type=MESH)

    r.pred_p[:, 96:, :] = jnp.zeros((2, 32, 128), F32)
    channels = target.shape[0]
    loads[0].wait()
    for m in range(MEMBERS_DEV):
        r.pred_p[m, :channels, :] = r.pred_in[pl.ds(m, channels, stride=MEMBERS_DEV), :]

    pl.semaphore_wait(barrier, len(greeted))

    pred_copies = []
    for o in range(1, 8):
        dest = (member + o) % 8
        pred_copies.append(start(remote(
            r.pred_p.at[:, pl.ds(pl.multiple_of(dest * CHANNEL_GROUP, CHANNEL_GROUP), CHANNEL_GROUP)],
            r.pred_g.at[member], r.pred_s.at[o - 1], r.pred_r.at[o - 1], (dest, slab),
        )))
    near, far = 2 - 2 * core, 2 * core
    far_device = (member, (slab + 15 + 2 * core) % 16)
    halo_near = start(remote(latent, r.lat.at[far], r.halo_s.at[0], r.halo_r.at[0], place.pair()))

    def halo_part(i):
        rows = pl.ds(i * 128, 128)
        return start(remote(
            latent.at[rows], r.lat.at[near, rows], r.halo_s.at[1 + i], r.halo_r.at[1 + i], far_device
        ))

    halo_far = [halo_part(0)]

    r.targ_p[...] = jnp.zeros((128, 128), F32)
    r.w_dec[...] = jnp.zeros((128, WIDTH), BF16)
    loads[2].wait()
    loads[3].wait()
    r.targ_p[:channels, :] = r.targ_in[...]
    r.w_dec[:channels, :] = r.w_out_in[...]
    lane = lax.broadcasted_iota(jnp.int32, (128, 128), 1)
    for h in range(2):
        r.mask[h] = jnp.where(lane // 64 == h, jnp.float32(1.0), jnp.float32(0.0)).astype(BF16)

    every = slice(0, ROWS)

    def normalise(block, keep, rows=every):
        xf = r.lat[block, rows, :].astype(F32)
        mean = jnp.mean(xf, axis=-1, keepdims=True)
        cent = xf - mean
        var = jnp.mean(cent * cent, axis=-1, keepdims=True)
        rstd = lax.rsqrt(var + 1e-05)
        norm = cent * rstd
        r.xn[block, rows, :] = norm.astype(BF16)
        if keep:
            r.norm[...] = norm
            r.rstd[...] = jnp.broadcast_to(rstd, (ROWS, 128))

    def project(block, begin, end, rows=every):
        for j in range(begin, end):
            piece = dot(r.xn[block, rows, :], r.w_in[:, j * HALF : (j + 1) * HALF]).astype(BF16)
            at = slice((j % 2) * HALF, (j % 2 + 1) * HALF)
            if j < 2:
                r.qx[block, rows, at] = piece * jnp.bfloat16(0.125)
            elif j < 4:
                r.kx[block, rows, at] = piece
            else:
                r.vx[block, rows, at] = piece

    loads[1].wait()
    normalise(1, True)
    for copy in loads[4:]:
        copy.wait()
    project(1, 0, 6)

    r.pred_g[member] = r.pred_p[:, pl.ds(pl.multiple_of(member * CHANNEL_GROUP, CHANNEL_GROUP), CHANNEL_GROUP), :]
    for copy in pred_copies:
        copy.wait_recv()
    y = [r.pred_g[i // 2, i % 2] for i in range(16)]
    pair_sum = [jnp.zeros((CHANNEL_GROUP, 128), F32) for _ in range(16)]
    for i in range(16):
        for k in range(i + 1, 16):
            s = sign_of(y[i], y[k])
            pair_sum[i] = pair_sum[i] + s
            pair_sum[k] = pair_sum[k] - s
    point = lax.broadcasted_iota(jnp.int32, (1, 128), 1)
    pweight = jnp.where(point < slab_count[0], area_weight[...], jnp.zeros((1, 128), F32))
    truth = r.targ_p[pl.ds(pl.multiple_of(member * CHANNEL_GROUP, CHANNEL_GROUP), CHANNEL_GROUP), :]
    for i in range(16):
        crps = pweight * (sign_of(y[i], truth) - pair_sum[i] / 15.0)
        r.crps_g[i // 2, i % 2] = crps.astype(BF16)
    own_group = pl.ds(pl.multiple_of(member * CHANNEL_GROUP, CHANNEL_GROUP), CHANNEL_GROUP)
    back_copies = []
    for o in range(1, 8):
        dest = (member + o) % 8
        back_copies.append(start(remote(
            r.crps_g.at[dest], r.cr.at[1, :, own_group], r.back_s.at[o - 1], r.back_r.at[o - 1], (dest, slab)
        )))
    r.cr[1, :, own_group, :] = r.crps_g[member]

    halo_far.append(halo_part(1))

    def decode(block):
        for m in range(2):
            turned = r.cr[block, m].T
            value = dot(turned, r.w_dec[...])
            at = slice(m * 128, m * 128 + 128)
            r.daf_b[block, at, :] = value.astype(BF16)
            if isinstance(block, int):
                r.daf[at, :] = value
                r.cr_rows[at, :] = turned

    def attend_back(block):
        for j in range(4):
            at = slice(j * GROUP, (j + 1) * GROUP)
            r.dx[block, :, at] = dot_nt(r.daf_b[block], r.w_back[at, :]).astype(BF16)

    def lay(value, targets, column):
        turned = value.T
        for ref, order in targets:
            for chunk, spot in enumerate(chunk_order(order)):
                ref[spot * 16 : spot * 16 + 16, column : column + ROWS] = turned[chunk * 16 : chunk * 16 + 16]

    xts = [(r.xt[0], ORDERS[0]), (r.xt[1], ORDERS[1]), (r.xt[2], ORDERS[2])]
    ats = [(r.at[0], ORDERS[1]), (r.at[1], ORDERS[2])]
    theirs = pl.multiple_of((1 - core) * HALF, HALF)
    high_rows = pl.ds(ROWS, ROWS)

    def give(i, src, dst):
        return start(remote(src, dst, r.pair_s.at[i], r.pair_r.at[i], place.pair()))

    halo_near.wait_recv()
    normalise(near, False)
    project(near, 0, 6)
    lay(r.xn[1], xts, 0)
    lay(r.xn[near], xts, ROWS)
    halo_far[0].wait_recv()
    member_rows = [slice(0, 128), slice(128, 256)]
    normalise(far, False, member_rows[0])
    project(far, 2, 6, member_rows[0])
    for copy in back_copies:
        copy.wait_recv()
    crh_near = start(remote(r.cr.at[1], r.cr.at[far], r.crh_s.at[0], r.crh_r.at[0], place.pair()))
    crh_far = start(remote(r.cr.at[1], r.cr.at[near], r.crh_s.at[1], r.crh_r.at[1], far_device))
    decode(1)
    pair_o = give(0, r.daf_b.at[1, :, pl.ds(theirs, HALF)], r.d_o.at[high_rows])
    attend_back(1)

    edge = [
        jnp.where(slab > 0, jnp.float32(0.0), jnp.float32(-1e30)),
        jnp.where(slab < 15, jnp.float32(0.0), jnp.float32(-1e30)),
    ]

    def spread(block):
        left, right = block[:, :128], block[:, 128:]
        zero = jnp.zeros((128, 128), BF16)
        return jnp.concatenate(
            [jnp.concatenate([left * r.mask[h], zero], axis=1) for h in range(2)]
            + [jnp.concatenate([zero, right * r.mask[h]], axis=1) for h in range(2)],
            axis=0,
        )

    def per_head(left, right):
        return jnp.concatenate(
            [dot(left[h * 64 : (h + 1) * 64], right[:, h * 128 : (h + 1) * 128]) for h in range(4)], axis=0
        ).T

    def group_cols(half, u, begin=0):
        return pl.ds(pl.multiple_of(begin + half * HALF + u * GROUP, GROUP), GROUP)

    def own_queries(m, half):
        rows = member_rows[m]
        for u in range(2):
            cols = group_cols(half, u)
            keys = jnp.concatenate([r.kx[b, rows, cols] for b in range(3)], axis=0)
            values = jnp.concatenate([r.vx[b, rows, cols] for b in range(3)], axis=0)
            q_b = spread(r.qx[1, rows, cols])
            d_b = spread(r.dx[1, rows, cols])
            scores = dot_nt(keys, q_b)
            scores = jnp.concatenate([scores[:128] + edge[0], scores[128:256], scores[256:] + edge[1]], axis=0)
            top = jnp.max(scores, axis=0, keepdims=True) * LOG2E
            e = jnp.exp2(scores * LOG2E - top)
            total = jnp.sum(e, axis=0, keepdims=True)
            prob = e * (1.0 / total)
            prob_b = prob.astype(BF16)
            dprob = dot_nt(values, d_b)
            delta = jnp.sum(dprob * prob, axis=0, keepdims=True)
            dscore = (prob * (dprob - delta)).astype(BF16)
            r.att[rows, cols] = per_head(values.T, prob_b).astype(BF16)
            r.dqkv[rows, cols] = (per_head(keys.T, dscore) * 0.125).astype(BF16)
            r.dk_acc[rows, cols] = dot(dscore[128:256], q_b)
            r.dv_acc[rows, cols] = dot(prob_b[128:256], d_b)
            r.stat[m, half, 2 * u : 2 * u + 1, :] = top + jnp.log2(total)
            r.stat[m, half, 2 * u + 1 : 2 * u + 2, :] = delta

    def send_stat(m):
        return [
            start(remote(
                r.stat.at[m], r.stat_n.at[core, m], r.sth_s.at[2 * m], r.sth_r.at[2 * m], place.pair()
            )),
            start(remote(
                r.stat.at[m], r.stat_n.at[1 - core, m], r.sth_s.at[2 * m + 1], r.sth_r.at[2 * m + 1], far_device
            )),
        ]

    r.stat[...] = jnp.zeros((2, 2, 8, 512), F32)
    own_queries(0, 1 - core)
    own_queries(0, core)
    sth = send_stat(0)
    halo_far[1].wait_recv()
    normalise(far, False, member_rows[1])
    project(far, 2, 6, member_rows[1])
    own_queries(1, 1 - core)
    own_half = pl.multiple_of(core * HALF, HALF)
    pair_q = give(1, r.dqkv.at[:, pl.ds(theirs, HALF)], r.d_q.at[high_rows])
    pair_a = [give(2, r.att.at[:, pl.ds(theirs, HALF)], r.att_o.at[:, pl.ds(theirs, HALF)])]
    own_queries(1, core)
    sth += send_stat(1)
    pair_a.append(give(3, r.att.at[:, pl.ds(own_half, HALF)], r.att_o.at[:, pl.ds(own_half, HALF)]))

    def mine(ref, at, begin):
        return jnp.where(core == 0, ref[at, begin : begin + HALF], ref[at, begin + HALF : begin + 2 * HALF])

    r.d_o[:ROWS] = mine(r.daf_b.at[1], slice(0, ROWS), 0)
    r.d_q[:ROWS] = mine(r.dqkv, slice(0, ROWS), 0)

    after = r.lat[1].astype(F32) + dot(r.att[...], r.w_back[...])
    lay(after.astype(BF16), [(r.ft, ORDERS[2])], 0)
    lay(r.att[...], ats, 0)
    for copy in pair_a:
        copy.wait_recv()
    lay(r.att_o[...], ats, ROWS)

    def terms(wave, p, dest):
        at = pl.ds(pl.multiple_of(dest * 256, 256), 256)
        if wave == 0:
            if p == 0:
                return [dot(r.xt[0][at, :], r.d_q[:, :384])]
            if p == 1:
                return [dot(r.xt[1][at, :], r.d_q[:, 384:]), dot(r.at[0][at, :], r.d_o[:, :256])]
            return [dot(r.at[1][at, :], r.d_o[:, 256:]), dot(r.ft[at, :], r.cr_rows[...])]
        if p == 0:
            return [dot(r.xt[0][at, :], r.d_k[:, :384])]
        if p == 1:
            return [dot(r.xt[1][at, :], r.d_k[:, 384:]), dot(r.xt[1][at, :], r.d_v[:, :256])]
        return [dot(r.xt[2][at, :], r.d_v[:, 256:])]

    def push(wave, p, slot, src, dst, device):
        slot = (wave * 3 + p) * 16 + slot
        return start(remote(src, dst, r.ring_s.at[slot], r.ring_r.at[slot], device))

    def neighbour(p, phase, offset):
        axis = ORDERS[p][phase]
        return place.partner(axis, place.ahead(axis, offset))

    def put(ref, index, values, dtype, rows=slice(None)):
        begin = 0
        for value in values:
            end = begin + value.shape[1]
            ref[index, rows, begin:end] = value.astype(dtype)
            begin = end

    def first(wave):
        copies = {}

        def go(p, slot, offset):
            copies[p, slot] = push(
                wave, p, slot, r.send1[wave][p].at[slot], r.recv1[wave][p].at[slot], neighbour(p, 0, offset)
            )

        for p in range(3):
            values = terms(wave, p, place.ahead(ORDERS[p][0], 2))
            put(r.send1[wave][p], 0, [v[:128] for v in values], BF16)
            put(r.send1[wave][p], 1, [v[128:] for v in values], BF16)
            go(p, 0, 1)
            go(p, 1, 3)
        for p in range(3):
            values = terms(wave, p, place.ahead(ORDERS[p][0], 1))
            put(r.send1[wave][p], 2, [v[128:] for v in values], BF16)
            put(r.hold[wave][p], 0, [v[:128] for v in values], F32)
            go(p, 2, 1)
            values = terms(wave, p, place.ahead(ORDERS[p][0], 3))
            put(r.send1[wave][p], 3, [v[:128] for v in values], BF16)
            put(r.hold[wave][p], 1, [v[128:] for v in values], F32)
            go(p, 3, 3)
        return copies

    def relay(wave, copies):
        for p in range(3):
            for half, offset in ((0, 1), (1, 3)):
                copies[p, half].wait_recv()
                r.send1[wave][p][4 + half] = (r.hold[wave][p][half] + r.recv1[wave][p][half].astype(F32)).astype(BF16)
                copies[p, 4 + half] = push(
                    wave, p, 4 + half, r.send1[wave][p].at[4 + half], r.recv1[wave][p].at[4 + half],
                    neighbour(p, 0, offset),
                )

    def own_terms(wave):
        for p in range(3):
            begin = 0
            for value in terms(wave, p, place.at[ORDERS[p][0]]):
                end = begin + value.shape[1]
                r.acc1[wave][p][:, begin:end] = value
                begin = end

    def second(wave, arrivals):
        copies = {}
        for p in range(3):
            acc, came = r.acc1[wave][p], r.recv1[wave][p]
            for slot in (2, 3, 4, 5):
                arrivals[p, slot].wait_recv()
            acc[:128] += came[3].astype(F32) + came[4].astype(F32)
            acc[128:] += came[2].astype(F32) + came[5].astype(F32)
            for offset in (2, 1, 3):
                dest = place.ahead(ORDERS[p][1], offset)
                r.send2[wave][p][offset - 1] = acc[pl.ds(pl.multiple_of(dest * 64, 64), 64), :].astype(BF16)
                copies[p, offset] = push(
                    wave, p, 5 + offset, r.send2[wave][p].at[offset - 1], r.recv2[wave][p].at[offset - 1],
                    neighbour(p, 1, offset),
                )
        return copies

    def third(wave, arrivals):
        copies = []
        for p in range(3):
            for offset in (1, 2, 3):
                arrivals[p, offset].wait_recv()
            own = r.acc1[wave][p][pl.ds(pl.multiple_of(place.at[ORDERS[p][1]] * 64, 64), 64), :]
            came = r.recv2[wave][p]
            r.acc2[wave][p][...] = own + (came[0].astype(F32) + came[1].astype(F32) + came[2].astype(F32))
            for offset in (2, 1, 3, 0):
                dest = place.ahead(ORDERS[p][2], offset)
                device = neighbour(p, 2, offset)
                for other in ((0, 1) if offset else (1,)):
                    side = core if other == 0 else 1 - core
                    slot = 3 + offset if other else offset - 1
                    src = r.acc2[wave][p].at[pl.ds(pl.multiple_of(dest * 16 + side * 8, 8), 8)]
                    to = (device[0], device[1] + (side - core))
                    copies.append(push(wave, p, 9 + slot, src, r.recv3[wave][p].at[slot], to))
        return copies

    def finish(wave, arrivals):
        for copy in arrivals:
            copy.wait_recv()
        own, other = [], []
        for p in range(3):
            came = r.recv3[wave][p]
            at = pl.ds(pl.multiple_of(place.at[ORDERS[p][2]] * 16 + core * 8, 8), 8)
            own.append(r.acc2[wave][p][at, :] + came[0] + came[1] + came[2])
            other.append(came[3] + came[4] + came[5] + came[6])
        return own, other

    def place_both(out, begin, own, other):
        width = own.shape[1]
        out[:, begin : begin + width] = jnp.where(core == 0, own, other)
        out[:, begin + HALF : begin + HALF + width] = jnp.where(core == 0, other, own)

    pair_o.wait_recv()
    pair_q.wait_recv()
    arrive0 = first(0)

    for side, copy in ((near, crh_near), (far, crh_far)):
        copy.wait_recv()
        decode(side)
        attend_back(side)
    project(far, 0, 2)

    def other_queries(half):
        for m in range(2):
            rows = member_rows[m]
            for u in range(2):
                cols = group_cols(half, u)
                keys = r.kx[1, rows, cols]
                values = r.vx[1, rows, cols]
                dk = r.dk_acc[rows, cols]
                dv = r.dv_acc[rows, cols]
                for side in range(2):
                    q_b = spread(r.qx[2 * side, rows, cols])
                    d_b = spread(r.dx[2 * side, rows, cols])
                    lse = r.stat_n[side, m, half, 2 * u : 2 * u + 1, :]
                    delta = r.stat_n[side, m, half, 2 * u + 1 : 2 * u + 2, :]
                    prob = jnp.exp2(dot_nt(keys, q_b) * LOG2E - (lse - edge[side]))
                    dscore = (prob * (dot_nt(values, d_b) - delta)).astype(BF16)
                    dk += dot(dscore, q_b)
                    dv += dot(prob.astype(BF16), d_b)
                r.dqkv[rows, group_cols(half, u, WIDTH)] = dk.astype(BF16)
                r.dqkv[rows, group_cols(half, u, 2 * WIDTH)] = dv.astype(BF16)

    for copy in sth:
        copy.wait_recv()
    other_queries(1 - core)
    pair_k = give(4, r.dqkv.at[:, pl.ds(pl.multiple_of(WIDTH + theirs, HALF), HALF)], r.d_k.at[high_rows])
    pair_v = give(5, r.dqkv.at[:, pl.ds(pl.multiple_of(2 * WIDTH + theirs, HALF), HALF)], r.d_v.at[high_rows])
    relay(0, arrive0)
    other_queries(core)
    r.d_k[:ROWS] = mine(r.dqkv, slice(0, ROWS), WIDTH)
    r.d_v[:ROWS] = mine(r.dqkv, slice(0, ROWS), 2 * WIDTH)
    pair_k.wait_recv()
    pair_v.wait_recv()
    arrive1 = first(1)
    own_terms(0)
    arrive0 = second(0, arrive0)
    own_terms(1)

    for j in range(4):
        at = slice(j * GROUP, (j + 1) * GROUP)
        r.dnorm[:, at] = dot_nt(r.dqkv[...], r.w_in[at, :])
    relay(1, arrive1)
    arrive0 = third(0, arrive0)
    dnorm = r.dnorm[...]
    norm = r.norm[...]
    dlayer = r.rstd[:, :1] * (
        dnorm
        - jnp.mean(dnorm, axis=-1, keepdims=True)
        - norm * jnp.mean(dnorm * norm, axis=-1, keepdims=True)
    )
    r.g_stage[...] = (r.daf[...] + dlayer).astype(BF16)
    stored = pltpu.make_async_copy(r.g_stage, g_latent, load.at[8])
    stored.start()

    arrive1 = second(1, arrive1)
    own, other = finish(0, arrive0)
    place_both(g_qkv, 0, own[0], other[0])
    place_both(g_qkv, 384, own[1][:, :128], other[1][:, :128])
    place_both(g_o, 0, own[1][:, 128:], other[1][:, 128:])
    place_both(g_o, 256, own[2][:, :256], other[2][:, :256])
    total = own[2][:, 256:] + other[2][:, 256:]
    g_out[...] = total[:, :channels]

    arrive1 = third(1, arrive1)
    own, other = finish(1, arrive1)
    place_both(g_qkv, WIDTH, own[0], other[0])
    place_both(g_qkv, WIDTH + 384, own[1][:, :128], other[1][:, :128])
    place_both(g_qkv, 2 * WIDTH, own[1][:, 128:], other[1][:, 128:])
    place_both(g_qkv, 2 * WIDTH + 256, own[2], other[2])
    stored.wait()
    for copy in sent:
        copy.wait_send()


def hand_over(*refs):
    copies = [pltpu.make_async_copy(refs[i], refs[4 + i], refs[8].at[i]) for i in range(4)]
    for copy in copies:
        copy.start()
    for copy in copies:
        copy.wait()


def on_device(latent, predictions, target, area_weight, slab_count, w_qkv, w_o, w_out):
    members_here, points, width = latent.shape
    channels = predictions.shape[1]
    rows = members_here * points
    vmem = pl.BlockSpec(memory_space=pltpu.VMEM)
    hbm = pl.BlockSpec(memory_space=pl.ANY)
    smem = pl.BlockSpec(memory_space=pltpu.SMEM)
    shapes = (
        jax.ShapeDtypeStruct((rows, width), BF16),
        jax.ShapeDtypeStruct((8, 3 * width), F32),
        jax.ShapeDtypeStruct((8, width), F32),
        jax.ShapeDtypeStruct((8, channels), F32),
    )
    grad_latent, grad_qkv, grad_o, grad_out = pl.pallas_call(
        kernel,
        out_shape=shapes,
        in_specs=[hbm, hbm, hbm, vmem, smem, hbm, hbm, hbm],
        out_specs=[hbm, vmem, vmem, vmem],
        scratch_shapes=SHAPES,
        compiler_params=pltpu.CompilerParams(
            collective_id=0, has_side_effects=True, vmem_limit_bytes=62 * 1024 * 1024
        ),
    )(
        latent.reshape(rows, width), predictions.transpose(1, 0, 2).reshape(members_here * channels, points), target, area_weight.reshape(1, points),
        slab_count, w_qkv, w_o, w_out.T,
    )
    grad_latent, grad_qkv, grad_o, grad_out = pl.pallas_call(
        hand_over,
        out_shape=shapes,
        in_specs=[hbm] * 4,
        out_specs=[hbm] * 4,
        scratch_shapes=[pltpu.SemaphoreType.DMA((4,))],
    )(grad_latent, grad_qkv, grad_o, grad_out)
    return grad_latent.reshape(latent.shape), grad_qkv, grad_o, grad_out


def solution(mesh):
    placed = (
        P("member", "space", None),
        P("member", None, "space"),
        P(None, "space"),
        P("space"),
        P("space"),
        P(),
        P(),
        P(),
    )
    return jax.shard_map(
        on_device,
        mesh=mesh,
        in_specs=placed,
        out_specs=(
            P("member", "space", None),
            P(("member", "space"), None),
            P(("member", "space"), None),
            P(("member", "space"), None),
        ),
        check_vma=False,
    )
```

```python
from types import SimpleNamespace

import jax
import jax.numpy as jnp
from jax import lax
from jax.experimental import pallas as pl
from jax.experimental.pallas import tpu as pltpu
from jax.sharding import PartitionSpec as P

RING = 4
MEMBERS_DEV = 2
ROWS = 256
WIDTH = 1024
HALF = 512
GROUP = 256
CHANNEL_GROUP = 16
LOG2E = 1.4426950408889634
F32 = jnp.float32
BF16 = jnp.bfloat16
MESH = pl.DeviceIdType.MESH

ORDERS = (("x", "y", "z"), ("y", "z", "x"), ("z", "x", "y"))
WIDTHS = ((384, 384, 384), (384, 384, 256))


class Place:
    def __init__(self):
        self.member = lax.axis_index("member")
        self.space = lax.axis_index("space")
        self.core = self.space % 2
        z_lo = (self.space // 2) % 2
        z_hi = self.member % 2
        self.at = {"x": self.space // 4, "y": self.member // 2, "z": z_hi * 2 + z_lo}

    def partner(self, axis, index):
        if axis == "x":
            return (self.member, index * 4 + self.space % 4)
        if axis == "y":
            return (index * 2 + self.member % 2, self.space)
        member = (self.member // 2) * 2 + index // 2
        return (member, (self.space // 4) * 4 + (index % 2) * 2 + self.core)

    def pair(self):
        return (self.member, self.space + 1 - 2 * self.core)

    def right(self):
        return (self.member, (self.space + 1) % 16)

    def left(self):
        return (self.member, (self.space + 15) % 16)

    def across(self, axis, offset):
        member, space = self.partner(axis, self.ahead(axis, offset))
        return (member, space + 1 - 2 * self.core)

    def ahead(self, axis, offset):
        return (self.at[axis] + offset) % RING


def chunk_order(order):
    where = []
    for y in range(4):
        for z_hi in range(2):
            for x in range(4):
                for z_lo in range(2):
                    digit = {"x": x, "y": y, "z": z_hi * 2 + z_lo}
                    a, b, c = (digit[name] for name in order)
                    where.append(a * 16 + b * 4 + c)
    return where


def remote(src, dst, send, recv, device):
    return pltpu.make_async_remote_copy(
        src_ref=src, dst_ref=dst, send_sem=send, recv_sem=recv, device_id=device, device_id_type=MESH
    )


def dot(a, b):
    return jnp.dot(a, b, preferred_element_type=F32)


def dot_nt(a, b):
    return lax.dot_general(a, b, (((1,), (1,)), ((), ())), preferred_element_type=F32)


def sign_of(a, b):
    one = jnp.float32(1.0)
    zero = jnp.float32(0.0)
    return jnp.where(a > b, one, zero) - jnp.where(a < b, one, zero)


def scratch():
    vmem = pltpu.VMEM
    dma = pltpu.SemaphoreType.DMA
    block3 = vmem((3, ROWS, WIDTH), BF16)
    rows_b = vmem((ROWS, WIDTH), BF16)
    rows_f = vmem((ROWS, WIDTH), F32)
    factor = vmem((2 * ROWS, HALF), BF16)
    turned = vmem((WIDTH, 2 * ROWS), BF16)

    def waves(*shape, dtype):
        return [[vmem((*shape, w), dtype) for w in widths] for widths in WIDTHS]

    return dict(
        w_in=vmem((WIDTH, 3 * WIDTH), BF16),
        w_back=vmem((WIDTH, WIDTH), BF16),
        w_dec=vmem((128, WIDTH), BF16),
        lat=block3, xn=block3, qx=block3, kx=block3, vx=block3, dx=block3,
        norm=rows_f, daf=rows_f, dk_acc=rows_f, dv_acc=rows_f, dnorm=rows_f,
        rstd=vmem((ROWS, 128), F32),
        daf_b=block3,
        att=rows_b, att_o=rows_b,
        dqkv=vmem((ROWS, 3 * WIDTH), BF16),
        mask=vmem((2, 128, 128), BF16),
        pred_in=vmem((200, 128), F32),
        targ_in=vmem((100, 128), F32),
        w_out_in=vmem((100, WIDTH), BF16),
        g_stage=vmem((ROWS, WIDTH), BF16),
        stat=vmem((2, 2, 8, 512), F32),
        stat_n=vmem((2, 2, 2, 8, 512), F32),
        pred_p=vmem((2, 128, 128), F32),
        targ_p=vmem((128, 128), F32),
        pred_g=vmem((8, 2, CHANNEL_GROUP, 128), F32),
        crps_g=vmem((8, 2, CHANNEL_GROUP, 128), BF16),
        cr=vmem((3, 2, 128, 128), BF16),
        cr_rows=vmem((ROWS, 128), BF16),
        d_q=factor, d_k=factor, d_v=factor, d_o=factor,
        xt=[turned] * 3,
        at=[turned] * 2,
        ft=vmem((WIDTH, ROWS), BF16),
        send1=waves(6, 128, dtype=BF16),
        recv1=waves(6, 128, dtype=BF16),
        hold=waves(2, 128, dtype=F32),
        acc1=waves(256, dtype=F32),
        send2=waves(3, 64, dtype=BF16),
        recv2=waves(3, 64, dtype=BF16),
        acc2=waves(64, dtype=F32),
        recv3=waves(7, 8, dtype=F32),
        load=dma((9,)),
        halo_s=dma((3,)), halo_r=dma((3,)),
        pred_s=dma((7,)), pred_r=dma((7,)),
        back_s=dma((7,)), back_r=dma((7,)),
        crh_s=dma((2,)), crh_r=dma((2,)),
        sth_s=dma((4,)), sth_r=dma((4,)),
        pair_s=dma((6,)), pair_r=dma((6,)),
        ring_s=dma((96,)), ring_r=dma((96,)),
    )


SHAPES, TREE = jax.tree.flatten(scratch())


def kernel(
    latent, predictions, target, area_weight, slab_count, w_qkv, w_o, w_out, g_latent, g_qkv, g_o, g_out, *buffers
):
    r = SimpleNamespace(**jax.tree.unflatten(TREE, buffers))
    place = Place()
    core, member, slab = place.core, place.member, place.space
    sent = []

    def start(copy):
        copy.start()
        sent.append(copy)
        return copy

    load = r.load
    moves = [(predictions, r.pred_in), (latent, r.lat.at[1]), (target, r.targ_in), (w_out, r.w_out_in)]
    for j in range(3):
        third_cols = pl.ds(j * WIDTH, WIDTH)
        moves.append((w_qkv.at[:, third_cols], r.w_in.at[:, third_cols]))
    moves.append((w_o, r.w_back))
    loads = [pltpu.make_async_copy(src, dst, load.at[i]) for i, (src, dst) in enumerate(moves)]
    for copy in loads:
        copy.start()

    barrier = pltpu.get_barrier_semaphore()
    greeted = [((member + o) % 8, slab) for o in range(1, 8)]
    greeted += [place.partner(axis, place.ahead(axis, o)) for axis in ("x", "z") for o in (1, 2, 3)]
    greeted += [place.right(), place.left()]
    greeted += [place.across(axis, o) for axis in ("x", "y", "z") for o in (1, 2, 3)]
    for device in greeted:
        pl.semaphore_signal(barrier, inc=1, device_id=device, device_id_type=MESH)

    r.pred_p[:, 96:, :] = jnp.zeros((2, 32, 128), F32)
    channels = target.shape[0]
    loads[0].wait()
    for m in range(MEMBERS_DEV):
        r.pred_p[m, :channels, :] = r.pred_in[pl.ds(m, channels, stride=MEMBERS_DEV), :]

    pl.semaphore_wait(barrier, len(greeted))

    pred_copies = []
    for o in range(1, 8):
        dest = (member + o) % 8
        pred_copies.append(start(remote(
            r.pred_p.at[:, pl.ds(pl.multiple_of(dest * CHANNEL_GROUP, CHANNEL_GROUP), CHANNEL_GROUP)],
            r.pred_g.at[member], r.pred_s.at[o - 1], r.pred_r.at[o - 1], (dest, slab),
        )))
    near, far = 2 - 2 * core, 2 * core
    far_device = (member, (slab + 15 + 2 * core) % 16)
    halo_near = start(remote(latent, r.lat.at[far], r.halo_s.at[0], r.halo_r.at[0], place.pair()))

    def halo_part(i):
        rows = pl.ds(i * 128, 128)
        return start(remote(
            latent.at[rows], r.lat.at[near, rows], r.halo_s.at[1 + i], r.halo_r.at[1 + i], far_device
        ))

    halo_far = [halo_part(0)]

    r.targ_p[...] = jnp.zeros((128, 128), F32)
    r.w_dec[...] = jnp.zeros((128, WIDTH), BF16)
    loads[2].wait()
    loads[3].wait()
    r.targ_p[:channels, :] = r.targ_in[...]
    r.w_dec[:channels, :] = r.w_out_in[...]
    lane = lax.broadcasted_iota(jnp.int32, (128, 128), 1)
    for h in range(2):
        r.mask[h] = jnp.where(lane // 64 == h, jnp.float32(1.0), jnp.float32(0.0)).astype(BF16)

    every = slice(0, ROWS)

    def normalise(block, keep, rows=every):
        xf = r.lat[block, rows, :].astype(F32)
        mean = jnp.mean(xf, axis=-1, keepdims=True)
        cent = xf - mean
        var = jnp.mean(cent * cent, axis=-1, keepdims=True)
        rstd = lax.rsqrt(var + 1e-05)
        norm = cent * rstd
        r.xn[block, rows, :] = norm.astype(BF16)
        if keep:
            r.norm[...] = norm
            r.rstd[...] = jnp.broadcast_to(rstd, (ROWS, 128))

    def project(block, begin, end, rows=every):
        for j in range(begin, end):
            piece = dot(r.xn[block, rows, :], r.w_in[:, j * HALF : (j + 1) * HALF]).astype(BF16)
            at = slice((j % 2) * HALF, (j % 2 + 1) * HALF)
            if j < 2:
                r.qx[block, rows, at] = piece * jnp.bfloat16(0.125)
            elif j < 4:
                r.kx[block, rows, at] = piece
            else:
                r.vx[block, rows, at] = piece

    loads[1].wait()
    normalise(1, True)
    for copy in loads[4:]:
        copy.wait()
    project(1, 0, 6)

    r.pred_g[member] = r.pred_p[:, pl.ds(pl.multiple_of(member * CHANNEL_GROUP, CHANNEL_GROUP), CHANNEL_GROUP), :]
    for copy in pred_copies:
        copy.wait_recv()
    y = [r.pred_g[i // 2, i % 2] for i in range(16)]
    pair_sum = [jnp.zeros((CHANNEL_GROUP, 128), F32) for _ in range(16)]
    for i in range(16):
        for k in range(i + 1, 16):
            s = sign_of(y[i], y[k])
            pair_sum[i] = pair_sum[i] + s
            pair_sum[k] = pair_sum[k] - s
    point = lax.broadcasted_iota(jnp.int32, (1, 128), 1)
    pweight = jnp.where(point < slab_count[0], area_weight[...], jnp.zeros((1, 128), F32))
    truth = r.targ_p[pl.ds(pl.multiple_of(member * CHANNEL_GROUP, CHANNEL_GROUP), CHANNEL_GROUP), :]
    for i in range(16):
        crps = pweight * (sign_of(y[i], truth) - pair_sum[i] / 15.0)
        r.crps_g[i // 2, i % 2] = crps.astype(BF16)
    own_group = pl.ds(pl.multiple_of(member * CHANNEL_GROUP, CHANNEL_GROUP), CHANNEL_GROUP)
    back_copies = []
    for o in range(1, 8):
        dest = (member + o) % 8
        back_copies.append(start(remote(
            r.crps_g.at[dest], r.cr.at[1, :, own_group], r.back_s.at[o - 1], r.back_r.at[o - 1], (dest, slab)
        )))
    r.cr[1, :, own_group, :] = r.crps_g[member]

    halo_far.append(halo_part(1))

    def decode(block):
        for m in range(2):
            turned = r.cr[block, m].T
            value = dot(turned, r.w_dec[...])
            at = slice(m * 128, m * 128 + 128)
            r.daf_b[block, at, :] = value.astype(BF16)
            if isinstance(block, int):
                r.daf[at, :] = value
                r.cr_rows[at, :] = turned

    def attend_back(block):
        for j in range(4):
            at = slice(j * GROUP, (j + 1) * GROUP)
            r.dx[block, :, at] = dot_nt(r.daf_b[block], r.w_back[at, :]).astype(BF16)

    def lay(value, targets, column):
        turned = value.T
        for ref, order in targets:
            for chunk, spot in enumerate(chunk_order(order)):
                ref[spot * 16 : spot * 16 + 16, column : column + ROWS] = turned[chunk * 16 : chunk * 16 + 16]

    xts = [(r.xt[0], ORDERS[0]), (r.xt[1], ORDERS[1]), (r.xt[2], ORDERS[2])]
    ats = [(r.at[0], ORDERS[1]), (r.at[1], ORDERS[2])]
    theirs = pl.multiple_of((1 - core) * HALF, HALF)
    high_rows = pl.ds(ROWS, ROWS)

    def give(i, src, dst):
        return start(remote(src, dst, r.pair_s.at[i], r.pair_r.at[i], place.pair()))

    halo_near.wait_recv()
    normalise(near, False)
    project(near, 0, 6)
    lay(r.xn[1], xts, 0)
    lay(r.xn[near], xts, ROWS)
    halo_far[0].wait_recv()
    member_rows = [slice(0, 128), slice(128, 256)]
    normalise(far, False, member_rows[0])
    project(far, 2, 6, member_rows[0])
    for copy in back_copies:
        copy.wait_recv()
    crh_near = start(remote(r.cr.at[1], r.cr.at[far], r.crh_s.at[0], r.crh_r.at[0], place.pair()))
    crh_far = start(remote(r.cr.at[1], r.cr.at[near], r.crh_s.at[1], r.crh_r.at[1], far_device))
    decode(1)
    pair_o = give(0, r.daf_b.at[1, :, pl.ds(theirs, HALF)], r.d_o.at[high_rows])
    attend_back(1)

    edge = [
        jnp.where(slab > 0, jnp.float32(0.0), jnp.float32(-1e30)),
        jnp.where(slab < 15, jnp.float32(0.0), jnp.float32(-1e30)),
    ]

    def spread(block):
        left, right = block[:, :128], block[:, 128:]
        zero = jnp.zeros((128, 128), BF16)
        return jnp.concatenate(
            [jnp.concatenate([left * r.mask[h], zero], axis=1) for h in range(2)]
            + [jnp.concatenate([zero, right * r.mask[h]], axis=1) for h in range(2)],
            axis=0,
        )

    def per_head(left, right):
        return jnp.concatenate(
            [dot(left[h * 64 : (h + 1) * 64], right[:, h * 128 : (h + 1) * 128]) for h in range(4)], axis=0
        ).T

    def group_cols(half, u, begin=0):
        return pl.ds(pl.multiple_of(begin + half * HALF + u * GROUP, GROUP), GROUP)

    def own_queries(m, half):
        rows = member_rows[m]
        for u in range(2):
            cols = group_cols(half, u)
            keys = jnp.concatenate([r.kx[b, rows, cols] for b in range(3)], axis=0)
            values = jnp.concatenate([r.vx[b, rows, cols] for b in range(3)], axis=0)
            q_b = spread(r.qx[1, rows, cols])
            d_b = spread(r.dx[1, rows, cols])
            scores = dot_nt(keys, q_b)
            scores = jnp.concatenate([scores[:128] + edge[0], scores[128:256], scores[256:] + edge[1]], axis=0)
            top = jnp.max(scores, axis=0, keepdims=True) * LOG2E
            e = jnp.exp2(scores * LOG2E - top)
            total = jnp.sum(e, axis=0, keepdims=True)
            prob = e * (1.0 / total)
            prob_b = prob.astype(BF16)
            dprob = dot_nt(values, d_b)
            delta = jnp.sum(dprob * prob, axis=0, keepdims=True)
            dscore = (prob * (dprob - delta)).astype(BF16)
            r.att[rows, cols] = per_head(values.T, prob_b).astype(BF16)
            r.dqkv[rows, cols] = (per_head(keys.T, dscore) * 0.125).astype(BF16)
            r.dk_acc[rows, cols] = dot(dscore[128:256], q_b)
            r.dv_acc[rows, cols] = dot(prob_b[128:256], d_b)
            r.stat[m, half, 2 * u : 2 * u + 1, :] = top + jnp.log2(total)
            r.stat[m, half, 2 * u + 1 : 2 * u + 2, :] = delta

    def send_stat(m):
        return [
            start(remote(
                r.stat.at[m], r.stat_n.at[core, m], r.sth_s.at[2 * m], r.sth_r.at[2 * m], place.pair()
            )),
            start(remote(
                r.stat.at[m], r.stat_n.at[1 - core, m], r.sth_s.at[2 * m + 1], r.sth_r.at[2 * m + 1], far_device
            )),
        ]

    r.stat[...] = jnp.zeros((2, 2, 8, 512), F32)
    own_queries(0, 1 - core)
    own_queries(0, core)
    sth = send_stat(0)
    halo_far[1].wait_recv()
    normalise(far, False, member_rows[1])
    project(far, 2, 6, member_rows[1])
    own_queries(1, 1 - core)
    own_half = pl.multiple_of(core * HALF, HALF)
    pair_q = give(1, r.dqkv.at[:, pl.ds(theirs, HALF)], r.d_q.at[high_rows])
    pair_a = [give(2, r.att.at[:, pl.ds(theirs, HALF)], r.att_o.at[:, pl.ds(theirs, HALF)])]
    own_queries(1, core)
    sth += send_stat(1)
    pair_a.append(give(3, r.att.at[:, pl.ds(own_half, HALF)], r.att_o.at[:, pl.ds(own_half, HALF)]))

    def mine(ref, at, begin):
        return jnp.where(core == 0, ref[at, begin : begin + HALF], ref[at, begin + HALF : begin + 2 * HALF])

    r.d_o[:ROWS] = mine(r.daf_b.at[1], slice(0, ROWS), 0)
    r.d_q[:ROWS] = mine(r.dqkv, slice(0, ROWS), 0)

    def terms(wave, p, dest):
        at = pl.ds(pl.multiple_of(dest * 256, 256), 256)
        if wave == 0:
            if p == 0:
                return [dot(r.xt[0][at, :], r.d_q[:, :384])]
            if p == 1:
                return [dot(r.xt[1][at, :], r.d_q[:, 384:]), dot(r.at[0][at, :], r.d_o[:, :256])]
            return [dot(r.at[1][at, :], r.d_o[:, 256:]), dot(r.ft[at, :], r.cr_rows[...])]
        if p == 0:
            return [dot(r.xt[0][at, :], r.d_k[:, :384])]
        if p == 1:
            return [dot(r.xt[1][at, :], r.d_k[:, 384:]), dot(r.xt[1][at, :], r.d_v[:, :256])]
        return [dot(r.xt[2][at, :], r.d_v[:, 256:])]

    def push(wave, p, slot, src, dst, device):
        slot = (wave * 3 + p) * 16 + slot
        return start(remote(src, dst, r.ring_s.at[slot], r.ring_r.at[slot], device))

    def neighbour(p, phase, offset):
        axis = ORDERS[p][phase]
        return place.partner(axis, place.ahead(axis, offset))

    def put(ref, index, values, dtype, rows=slice(None)):
        begin = 0
        for value in values:
            end = begin + value.shape[1]
            ref[index, rows, begin:end] = value.astype(dtype)
            begin = end

    def go(wave, copies, p, slot, offset):
        copies[p, slot] = push(
            wave, p, slot, r.send1[wave][p].at[slot], r.recv1[wave][p].at[slot], neighbour(p, 0, offset)
        )

    def first_relayed(wave, copies, p):
        values = terms(wave, p, place.ahead(ORDERS[p][0], 2))
        put(r.send1[wave][p], 0, [v[:128] for v in values], BF16)
        put(r.send1[wave][p], 1, [v[128:] for v in values], BF16)
        go(wave, copies, p, 0, 1)
        go(wave, copies, p, 1, 3)

    def first_direct(wave, copies, p):
        values = terms(wave, p, place.ahead(ORDERS[p][0], 1))
        put(r.send1[wave][p], 2, [v[128:] for v in values], BF16)
        put(r.hold[wave][p], 0, [v[:128] for v in values], F32)
        go(wave, copies, p, 2, 1)
        values = terms(wave, p, place.ahead(ORDERS[p][0], 3))
        put(r.send1[wave][p], 3, [v[:128] for v in values], BF16)
        put(r.hold[wave][p], 1, [v[128:] for v in values], F32)
        go(wave, copies, p, 3, 3)

    def relay(wave, copies, parts=(0, 1, 2)):
        for p in parts:
            for half, offset in ((0, 1), (1, 3)):
                copies[p, half].wait_recv()
                r.send1[wave][p][4 + half] = (r.hold[wave][p][half] + r.recv1[wave][p][half].astype(F32)).astype(BF16)
                copies[p, 4 + half] = push(
                    wave, p, 4 + half, r.send1[wave][p].at[4 + half], r.recv1[wave][p].at[4 + half],
                    neighbour(p, 0, offset),
                )

    def own_terms(wave):
        for p in range(3):
            begin = 0
            for value in terms(wave, p, place.at[ORDERS[p][0]]):
                end = begin + value.shape[1]
                r.acc1[wave][p][:, begin:end] = value
                begin = end

    def second(wave, arrivals):
        copies = {}
        for p in range(3):
            acc, came = r.acc1[wave][p], r.recv1[wave][p]
            for slot in (2, 3, 4, 5):
                arrivals[p, slot].wait_recv()
            acc[:128] += came[3].astype(F32) + came[4].astype(F32)
            acc[128:] += came[2].astype(F32) + came[5].astype(F32)
            for offset in (2, 1, 3):
                dest = place.ahead(ORDERS[p][1], offset)
                r.send2[wave][p][offset - 1] = acc[pl.ds(pl.multiple_of(dest * 64, 64), 64), :].astype(BF16)
                copies[p, offset] = push(
                    wave, p, 5 + offset, r.send2[wave][p].at[offset - 1], r.recv2[wave][p].at[offset - 1],
                    neighbour(p, 1, offset),
                )
        return copies

    def third(wave, arrivals):
        copies = []
        for p in range(3):
            for offset in (1, 2, 3):
                arrivals[p, offset].wait_recv()
            own = r.acc1[wave][p][pl.ds(pl.multiple_of(place.at[ORDERS[p][1]] * 64, 64), 64), :]
            came = r.recv2[wave][p]
            r.acc2[wave][p][...] = own + (came[0].astype(F32) + came[1].astype(F32) + came[2].astype(F32))
            for offset in (2, 1, 3, 0):
                dest = place.ahead(ORDERS[p][2], offset)
                device = neighbour(p, 2, offset)
                for other in ((0, 1) if offset else (1,)):
                    side = core if other == 0 else 1 - core
                    slot = 3 + offset if other else offset - 1
                    src = r.acc2[wave][p].at[pl.ds(pl.multiple_of(dest * 16 + side * 8, 8), 8)]
                    to = (device[0], device[1] + (side - core))
                    copies.append(push(wave, p, 9 + slot, src, r.recv3[wave][p].at[slot], to))
        return copies

    def finish(wave, arrivals):
        for copy in arrivals:
            copy.wait_recv()
        own, other = [], []
        for p in range(3):
            came = r.recv3[wave][p]
            at = pl.ds(pl.multiple_of(place.at[ORDERS[p][2]] * 16 + core * 8, 8), 8)
            own.append(r.acc2[wave][p][at, :] + came[0] + came[1] + came[2])
            other.append(came[3] + came[4] + came[5] + came[6])
        return own, other

    def place_both(out, begin, own, other):
        width = own.shape[1]
        out[:, begin : begin + width] = jnp.where(core == 0, own, other)
        out[:, begin + HALF : begin + HALF + width] = jnp.where(core == 0, other, own)

    arrive0 = {}
    pair_q.wait_recv()
    first_relayed(0, arrive0, 0)
    first_direct(0, arrive0, 0)
    lay(r.att[...], ats, 0)
    pair_o.wait_recv()
    for copy in pair_a:
        copy.wait_recv()
    lay(r.att_o[...], ats, ROWS)
    first_relayed(0, arrive0, 1)
    after = r.lat[1].astype(F32) + dot(r.att[...], r.w_back[...])
    lay(after.astype(BF16), [(r.ft, ORDERS[2])], 0)
    first_relayed(0, arrive0, 2)
    first_direct(0, arrive0, 1)
    first_direct(0, arrive0, 2)

    for side, copy in ((near, crh_near), (far, crh_far)):
        copy.wait_recv()
        decode(side)
        attend_back(side)
    project(far, 0, 2)

    def other_queries(half, members=(0, 1)):
        for m in members:
            rows = member_rows[m]
            for u in range(2):
                cols = group_cols(half, u)
                keys = r.kx[1, rows, cols]
                values = r.vx[1, rows, cols]
                dk = r.dk_acc[rows, cols]
                dv = r.dv_acc[rows, cols]
                for side in range(2):
                    q_b = spread(r.qx[2 * side, rows, cols])
                    d_b = spread(r.dx[2 * side, rows, cols])
                    lse = r.stat_n[side, m, half, 2 * u : 2 * u + 1, :]
                    delta = r.stat_n[side, m, half, 2 * u + 1 : 2 * u + 2, :]
                    prob = jnp.exp2(dot_nt(keys, q_b) * LOG2E - (lse - edge[side]))
                    dscore = (prob * (dot_nt(values, d_b) - delta)).astype(BF16)
                    dk += dot(dscore, q_b)
                    dv += dot(prob.astype(BF16), d_b)
                r.dqkv[rows, group_cols(half, u, WIDTH)] = dk.astype(BF16)
                r.dqkv[rows, group_cols(half, u, 2 * WIDTH)] = dv.astype(BF16)

    for copy in sth:
        copy.wait_recv()
    relay(0, arrive0, (0,))
    other_queries(1 - core, (0,))
    relay(0, arrive0, (1,))
    other_queries(1 - core, (1,))
    pair_k = give(4, r.dqkv.at[:, pl.ds(pl.multiple_of(WIDTH + theirs, HALF), HALF)], r.d_k.at[high_rows])
    pair_v = give(5, r.dqkv.at[:, pl.ds(pl.multiple_of(2 * WIDTH + theirs, HALF), HALF)], r.d_v.at[high_rows])
    relay(0, arrive0, (2,))
    other_queries(core)
    r.d_k[:ROWS] = mine(r.dqkv, slice(0, ROWS), WIDTH)
    r.d_v[:ROWS] = mine(r.dqkv, slice(0, ROWS), 2 * WIDTH)
    pair_k.wait_recv()
    pair_v.wait_recv()
    arrive1 = {}
    for p in range(3):
        first_relayed(1, arrive1, p)
    for p in range(3):
        first_direct(1, arrive1, p)
    own_terms(0)
    arrive0 = second(0, arrive0)
    own_terms(1)

    for j in range(4):
        at = slice(j * GROUP, (j + 1) * GROUP)
        r.dnorm[:, at] = dot_nt(r.dqkv[...], r.w_in[at, :])
    relay(1, arrive1)
    arrive0 = third(0, arrive0)
    dnorm = r.dnorm[...]
    norm = r.norm[...]
    dlayer = r.rstd[:, :1] * (
        dnorm
        - jnp.mean(dnorm, axis=-1, keepdims=True)
        - norm * jnp.mean(dnorm * norm, axis=-1, keepdims=True)
    )
    r.g_stage[...] = (r.daf[...] + dlayer).astype(BF16)
    stored = pltpu.make_async_copy(r.g_stage, g_latent, load.at[8])
    stored.start()

    arrive1 = second(1, arrive1)
    own, other = finish(0, arrive0)
    place_both(g_qkv, 0, own[0], other[0])
    place_both(g_qkv, 384, own[1][:, :128], other[1][:, :128])
    place_both(g_o, 0, own[1][:, 128:], other[1][:, 128:])
    place_both(g_o, 256, own[2][:, :256], other[2][:, :256])
    total = own[2][:, 256:] + other[2][:, 256:]
    g_out[...] = total[:, :channels]

    arrive1 = third(1, arrive1)
    own, other = finish(1, arrive1)
    place_both(g_qkv, WIDTH, own[0], other[0])
    place_both(g_qkv, WIDTH + 384, own[1][:, :128], other[1][:, :128])
    place_both(g_qkv, 2 * WIDTH, own[1][:, 128:], other[1][:, 128:])
    place_both(g_qkv, 2 * WIDTH + 256, own[2], other[2])
    stored.wait()
    for copy in sent:
        copy.wait_send()


def hand_over(*refs):
    for source, target in zip(refs[:4], refs[4:]):
        target[...] = source[...]


def on_device(latent, predictions, target, area_weight, slab_count, w_qkv, w_o, w_out):
    members_here, points, width = latent.shape
    channels = predictions.shape[1]
    rows = members_here * points
    vmem = pl.BlockSpec(memory_space=pltpu.VMEM)
    hbm = pl.BlockSpec(memory_space=pl.ANY)
    smem = pl.BlockSpec(memory_space=pltpu.SMEM)
    shapes = (
        jax.ShapeDtypeStruct((rows, width), BF16),
        jax.ShapeDtypeStruct((8, 3 * width), F32),
        jax.ShapeDtypeStruct((8, width), F32),
        jax.ShapeDtypeStruct((8, channels), F32),
    )
    grad_latent, grad_qkv, grad_o, grad_out = pl.pallas_call(
        kernel,
        out_shape=shapes,
        in_specs=[hbm, hbm, hbm, vmem, smem, hbm, hbm, hbm],
        out_specs=[hbm, vmem, vmem, vmem],
        scratch_shapes=SHAPES,
        compiler_params=pltpu.CompilerParams(
            collective_id=0, has_side_effects=True, vmem_limit_bytes=62 * 1024 * 1024
        ),
    )(
        latent.reshape(rows, width), predictions.transpose(1, 0, 2).reshape(members_here * channels, points), target, area_weight.reshape(1, points),
        slab_count, w_qkv, w_o, w_out.T,
    )
    grad_latent, grad_qkv, grad_o, grad_out = pl.pallas_call(
        hand_over,
        out_shape=shapes,
        in_specs=[vmem] * 4,
        out_specs=[vmem] * 4,
    )(grad_latent, grad_qkv, grad_o, grad_out)
    return grad_latent.reshape(latent.shape), grad_qkv, grad_o, grad_out


def solution(mesh):
    placed = (
        P("member", "space", None),
        P("member", None, "space"),
        P(None, "space"),
        P("space"),
        P("space"),
        P(),
        P(),
        P(),
    )
    return jax.shard_map(
        on_device,
        mesh=mesh,
        in_specs=placed,
        out_specs=(
            P("member", "space", None),
            P(("member", "space"), None),
            P(("member", "space"), None),
            P(("member", "space"), None),
        ),
        check_vma=False,
    )
```

```python
from types import SimpleNamespace

import jax
import jax.numpy as jnp
from jax import lax
from jax.experimental import pallas as pl
from jax.experimental.pallas import tpu as pltpu
from jax.sharding import PartitionSpec as P

RING = 4
MEMBERS_DEV = 2
ROWS = 256
WIDTH = 1024
HALF = 512
GROUP = 256
CHANNEL_GROUP = 16
LOG2E = 1.4426950408889634
F32 = jnp.float32
BF16 = jnp.bfloat16
MESH = pl.DeviceIdType.MESH

ORDERS = (("x", "y", "z"), ("y", "z", "x"), ("z", "x", "y"))
WIDTHS = ((384, 384, 384), (384, 384, 256))


class Place:
    def __init__(self):
        self.member = lax.axis_index("member")
        self.space = lax.axis_index("space")
        self.core = self.space % 2
        z_lo = (self.space // 2) % 2
        z_hi = self.member % 2
        self.at = {"x": self.space // 4, "y": self.member // 2, "z": z_hi * 2 + z_lo}

    def partner(self, axis, index):
        if axis == "x":
            return (self.member, index * 4 + self.space % 4)
        if axis == "y":
            return (index * 2 + self.member % 2, self.space)
        member = (self.member // 2) * 2 + index // 2
        return (member, (self.space // 4) * 4 + (index % 2) * 2 + self.core)

    def pair(self):
        return (self.member, self.space + 1 - 2 * self.core)

    def right(self):
        return (self.member, (self.space + 1) % 16)

    def left(self):
        return (self.member, (self.space + 15) % 16)

    def across(self, axis, offset):
        member, space = self.partner(axis, self.ahead(axis, offset))
        return (member, space + 1 - 2 * self.core)

    def ahead(self, axis, offset):
        return (self.at[axis] + offset) % RING


def chunk_order(order):
    where = []
    for y in range(4):
        for z_hi in range(2):
            for x in range(4):
                for z_lo in range(2):
                    digit = {"x": x, "y": y, "z": z_hi * 2 + z_lo}
                    a, b, c = (digit[name] for name in order)
                    where.append(a * 16 + b * 4 + c)
    return where


def remote(src, dst, send, recv, device):
    return pltpu.make_async_remote_copy(
        src_ref=src, dst_ref=dst, send_sem=send, recv_sem=recv, device_id=device, device_id_type=MESH
    )


def dot(a, b):
    return jnp.dot(a, b, preferred_element_type=F32)


def dot_nt(a, b):
    return lax.dot_general(a, b, (((1,), (1,)), ((), ())), preferred_element_type=F32)


def sign_of(a, b):
    one = jnp.float32(1.0)
    zero = jnp.float32(0.0)
    return jnp.where(a > b, one, zero) - jnp.where(a < b, one, zero)


def scratch():
    vmem = pltpu.VMEM
    dma = pltpu.SemaphoreType.DMA
    block3 = vmem((3, ROWS, WIDTH), BF16)
    rows_b = vmem((ROWS, WIDTH), BF16)
    rows_f = vmem((ROWS, WIDTH), F32)
    factor = vmem((2 * ROWS, HALF), BF16)
    turned = vmem((WIDTH, 2 * ROWS), BF16)

    def waves(*shape, dtype):
        return [[vmem((*shape, w), dtype) for w in widths] for widths in WIDTHS]

    return dict(
        w_in=vmem((WIDTH, 3 * WIDTH), BF16),
        w_back=vmem((WIDTH, WIDTH), BF16),
        w_dec=vmem((128, WIDTH), BF16),
        lat=block3, xn=block3, qx=block3, kx=block3, vx=block3, dx=block3,
        norm=rows_f, daf=rows_f, dk_acc=rows_f, dv_acc=rows_f, dnorm=rows_f,
        rstd=vmem((ROWS, 128), F32),
        daf_b=block3,
        att=rows_b, att_o=rows_b,
        dqkv=vmem((ROWS, 3 * WIDTH), BF16),
        mask=vmem((2, 128, 128), BF16),
        pred_in=vmem((200, 128), F32),
        targ_in=vmem((100, 128), F32),
        w_out_in=vmem((100, WIDTH), BF16),
        g_stage=vmem((ROWS, WIDTH), BF16),
        stat=vmem((2, 2, 8, 512), F32),
        stat_n=vmem((2, 2, 2, 8, 512), F32),
        pred_p=vmem((2, 128, 128), F32),
        targ_p=vmem((128, 128), F32),
        pred_g=vmem((8, 2, CHANNEL_GROUP, 128), F32),
        crps_g=vmem((8, 2, CHANNEL_GROUP, 128), BF16),
        cr=vmem((3, 2, 128, 128), BF16),
        cr_rows=vmem((ROWS, 128), BF16),
        d_q=factor, d_k=factor, d_v=factor, d_o=factor,
        xt=[turned] * 3,
        at=[turned] * 2,
        ft=vmem((WIDTH, ROWS), BF16),
        send1=waves(6, 128, dtype=BF16),
        recv1=waves(6, 128, dtype=BF16),
        hold=waves(2, 128, dtype=F32),
        acc1=waves(256, dtype=F32),
        send2=waves(3, 64, dtype=BF16),
        recv2=waves(3, 64, dtype=BF16),
        acc2=waves(64, dtype=F32),
        recv3=waves(7, 8, dtype=F32),
        load=dma((9,)),
        halo_s=dma((3,)), halo_r=dma((3,)),
        pred_s=dma((7,)), pred_r=dma((7,)),
        back_s=dma((7,)), back_r=dma((7,)),
        crh_s=dma((2,)), crh_r=dma((2,)),
        sth_s=dma((4,)), sth_r=dma((4,)),
        pair_s=dma((6,)), pair_r=dma((6,)),
        ring_s=dma((96,)), ring_r=dma((96,)),
    )


SHAPES, TREE = jax.tree.flatten(scratch())


def kernel(
    latent, predictions, target, area_weight, slab_count, w_qkv, w_o, w_out, g_latent, g_qkv, g_o, g_out, *buffers
):
    r = SimpleNamespace(**jax.tree.unflatten(TREE, buffers))
    place = Place()
    core, member, slab = place.core, place.member, place.space
    sent = []

    def start(copy):
        copy.start()
        sent.append(copy)
        return copy

    load = r.load
    moves = [(predictions, r.pred_in), (latent, r.lat.at[1]), (target, r.targ_in), (w_out, r.w_out_in)]
    for j in range(3):
        third_cols = pl.ds(j * WIDTH, WIDTH)
        moves.append((w_qkv.at[:, third_cols], r.w_in.at[:, third_cols]))
    moves.append((w_o, r.w_back))
    loads = [pltpu.make_async_copy(src, dst, load.at[i]) for i, (src, dst) in enumerate(moves)]
    for copy in loads:
        copy.start()

    barrier = pltpu.get_barrier_semaphore()
    greeted = [((member + o) % 8, slab) for o in range(1, 8)]
    greeted += [place.partner(axis, place.ahead(axis, o)) for axis in ("x", "z") for o in (1, 2, 3)]
    greeted += [place.right(), place.left()]
    greeted += [place.across(axis, o) for axis in ("x", "y", "z") for o in (1, 2, 3)]
    for device in greeted:
        pl.semaphore_signal(barrier, inc=1, device_id=device, device_id_type=MESH)

    r.pred_p[:, 96:, :] = jnp.zeros((2, 32, 128), F32)
    channels = target.shape[0]
    loads[0].wait()
    for m in range(MEMBERS_DEV):
        r.pred_p[m, :channels, :] = r.pred_in[pl.ds(m, channels, stride=MEMBERS_DEV), :]

    pl.semaphore_wait(barrier, len(greeted))

    pred_copies = []
    for o in range(1, 8):
        dest = (member + o) % 8
        pred_copies.append(start(remote(
            r.pred_p.at[:, pl.ds(pl.multiple_of(dest * CHANNEL_GROUP, CHANNEL_GROUP), CHANNEL_GROUP)],
            r.pred_g.at[member], r.pred_s.at[o - 1], r.pred_r.at[o - 1], (dest, slab),
        )))
    near, far = 2 - 2 * core, 2 * core
    far_device = (member, (slab + 15 + 2 * core) % 16)
    halo_near = start(remote(latent, r.lat.at[far], r.halo_s.at[0], r.halo_r.at[0], place.pair()))

    def halo_part(i):
        rows = pl.ds(i * 128, 128)
        return start(remote(
            latent.at[rows], r.lat.at[near, rows], r.halo_s.at[1 + i], r.halo_r.at[1 + i], far_device
        ))

    halo_far = [halo_part(0)]

    r.targ_p[...] = jnp.zeros((128, 128), F32)
    r.w_dec[...] = jnp.zeros((128, WIDTH), BF16)
    loads[2].wait()
    loads[3].wait()
    r.targ_p[:channels, :] = r.targ_in[...]
    r.w_dec[:channels, :] = r.w_out_in[...]
    lane = lax.broadcasted_iota(jnp.int32, (128, 128), 1)
    for h in range(2):
        r.mask[h] = jnp.where(lane // 64 == h, jnp.float32(1.0), jnp.float32(0.0)).astype(BF16)

    every = slice(0, ROWS)

    def normalise(block, keep, rows=every):
        xf = r.lat[block, rows, :].astype(F32)
        mean = jnp.mean(xf, axis=-1, keepdims=True)
        cent = xf - mean
        var = jnp.mean(cent * cent, axis=-1, keepdims=True)
        rstd = lax.rsqrt(var + 1e-05)
        norm = cent * rstd
        r.xn[block, rows, :] = norm.astype(BF16)
        if keep:
            r.norm[...] = norm
            r.rstd[...] = jnp.broadcast_to(rstd, (ROWS, 128))

    def project(block, begin, end, rows=every):
        for j in range(begin, end):
            piece = dot(r.xn[block, rows, :], r.w_in[:, j * HALF : (j + 1) * HALF]).astype(BF16)
            at = slice((j % 2) * HALF, (j % 2 + 1) * HALF)
            if j < 2:
                r.qx[block, rows, at] = piece * jnp.bfloat16(0.125)
            elif j < 4:
                r.kx[block, rows, at] = piece
            else:
                r.vx[block, rows, at] = piece

    loads[1].wait()
    normalise(1, True)
    for copy in loads[4:]:
        copy.wait()
    project(1, 0, 6)

    r.pred_g[member] = r.pred_p[:, pl.ds(pl.multiple_of(member * CHANNEL_GROUP, CHANNEL_GROUP), CHANNEL_GROUP), :]
    for copy in pred_copies:
        copy.wait_recv()
    y = [r.pred_g[i // 2, i % 2] for i in range(16)]
    pair_sum = [jnp.zeros((CHANNEL_GROUP, 128), F32) for _ in range(16)]
    for i in range(16):
        for k in range(i + 1, 16):
            s = sign_of(y[i], y[k])
            pair_sum[i] = pair_sum[i] + s
            pair_sum[k] = pair_sum[k] - s
    point = lax.broadcasted_iota(jnp.int32, (1, 128), 1)
    pweight = jnp.where(point < slab_count[0], area_weight[...], jnp.zeros((1, 128), F32))
    truth = r.targ_p[pl.ds(pl.multiple_of(member * CHANNEL_GROUP, CHANNEL_GROUP), CHANNEL_GROUP), :]
    for i in range(16):
        crps = pweight * (sign_of(y[i], truth) - pair_sum[i] / 15.0)
        r.crps_g[i // 2, i % 2] = crps.astype(BF16)
    own_group = pl.ds(pl.multiple_of(member * CHANNEL_GROUP, CHANNEL_GROUP), CHANNEL_GROUP)
    back_copies = []
    for o in range(1, 8):
        dest = (member + o) % 8
        back_copies.append(start(remote(
            r.crps_g.at[dest], r.cr.at[1, :, own_group], r.back_s.at[o - 1], r.back_r.at[o - 1], (dest, slab)
        )))
    r.cr[1, :, own_group, :] = r.crps_g[member]

    halo_far.append(halo_part(1))

    def decode(block):
        for m in range(2):
            turned = r.cr[block, m].T
            value = dot(turned, r.w_dec[...])
            at = slice(m * 128, m * 128 + 128)
            r.daf_b[block, at, :] = value.astype(BF16)
            if isinstance(block, int):
                r.daf[at, :] = value
                r.cr_rows[at, :] = turned

    def attend_back(block):
        for j in range(4):
            at = slice(j * GROUP, (j + 1) * GROUP)
            r.dx[block, :, at] = dot_nt(r.daf_b[block], r.w_back[at, :]).astype(BF16)

    def lay(value, targets, column):
        turned = value.T
        for ref, order in targets:
            for chunk, spot in enumerate(chunk_order(order)):
                ref[spot * 16 : spot * 16 + 16, column : column + ROWS] = turned[chunk * 16 : chunk * 16 + 16]

    xts = [(r.xt[0], ORDERS[0]), (r.xt[1], ORDERS[1]), (r.xt[2], ORDERS[2])]
    ats = [(r.at[0], ORDERS[1]), (r.at[1], ORDERS[2])]
    theirs = pl.multiple_of((1 - core) * HALF, HALF)
    high_rows = pl.ds(ROWS, ROWS)

    def give(i, src, dst):
        return start(remote(src, dst, r.pair_s.at[i], r.pair_r.at[i], place.pair()))

    halo_near.wait_recv()
    normalise(near, False)
    project(near, 0, 6)
    lay(r.xn[1], xts, 0)
    lay(r.xn[near], xts, ROWS)
    halo_far[0].wait_recv()
    member_rows = [slice(0, 128), slice(128, 256)]
    normalise(far, False, member_rows[0])
    project(far, 2, 6, member_rows[0])
    for copy in back_copies:
        copy.wait_recv()
    crh_near = start(remote(r.cr.at[1], r.cr.at[far], r.crh_s.at[0], r.crh_r.at[0], place.pair()))
    crh_far = start(remote(r.cr.at[1], r.cr.at[near], r.crh_s.at[1], r.crh_r.at[1], far_device))
    decode(1)
    pair_o = give(0, r.daf_b.at[1, :, pl.ds(theirs, HALF)], r.d_o.at[high_rows])
    attend_back(1)

    edge = [
        jnp.where(slab > 0, jnp.float32(0.0), jnp.float32(-1e30)),
        jnp.where(slab < 15, jnp.float32(0.0), jnp.float32(-1e30)),
    ]

    def spread(block):
        left, right = block[:, :128], block[:, 128:]
        zero = jnp.zeros((128, 128), BF16)
        return jnp.concatenate(
            [jnp.concatenate([left * r.mask[h], zero], axis=1) for h in range(2)]
            + [jnp.concatenate([zero, right * r.mask[h]], axis=1) for h in range(2)],
            axis=0,
        )

    def per_head(left, right):
        return jnp.concatenate(
            [dot(left[h * 64 : (h + 1) * 64], right[:, h * 128 : (h + 1) * 128]) for h in range(4)], axis=0
        ).T

    def group_cols(half, u, begin=0):
        return pl.ds(pl.multiple_of(begin + half * HALF + u * GROUP, GROUP), GROUP)

    def own_queries(m, half):
        rows = member_rows[m]
        chains = []
        for u in range(2):
            cols = group_cols(half, u)
            keys = jnp.concatenate([r.kx[b, rows, cols] for b in range(3)], axis=0)
            values = jnp.concatenate([r.vx[b, rows, cols] for b in range(3)], axis=0)
            q_b = spread(r.qx[1, rows, cols])
            d_b = spread(r.dx[1, rows, cols])
            chains.append((cols, keys, values, q_b, d_b, dot_nt(keys, q_b), dot_nt(values, d_b)))
        probs = []
        for u, (cols, keys, values, q_b, d_b, scores, dprob) in enumerate(chains):
            scores = jnp.concatenate([scores[:128] + edge[0], scores[128:256], scores[256:] + edge[1]], axis=0)
            top = jnp.max(scores, axis=0, keepdims=True) * LOG2E
            e = jnp.exp2(scores * LOG2E - top)
            total = jnp.sum(e, axis=0, keepdims=True)
            prob = e * (1.0 / total)
            delta = jnp.sum(dprob * prob, axis=0, keepdims=True)
            dscore = (prob * (dprob - delta)).astype(BF16)
            probs.append((prob.astype(BF16), dscore))
            r.stat[m, half, 2 * u : 2 * u + 1, :] = top + jnp.log2(total)
            r.stat[m, half, 2 * u + 1 : 2 * u + 2, :] = delta
        for (cols, keys, values, q_b, d_b, _, _), (prob_b, dscore) in zip(chains, probs):
            r.att[rows, cols] = per_head(values.T, prob_b).astype(BF16)
            r.dqkv[rows, cols] = (per_head(keys.T, dscore) * 0.125).astype(BF16)
            r.dk_acc[rows, cols] = dot(dscore[128:256], q_b)
            r.dv_acc[rows, cols] = dot(prob_b[128:256], d_b)

    def send_stat(m):
        return [
            start(remote(
                r.stat.at[m], r.stat_n.at[core, m], r.sth_s.at[2 * m], r.sth_r.at[2 * m], place.pair()
            )),
            start(remote(
                r.stat.at[m], r.stat_n.at[1 - core, m], r.sth_s.at[2 * m + 1], r.sth_r.at[2 * m + 1], far_device
            )),
        ]

    r.stat[...] = jnp.zeros((2, 2, 8, 512), F32)
    own_queries(0, 1 - core)
    own_queries(0, core)
    sth = send_stat(0)
    halo_far[1].wait_recv()
    normalise(far, False, member_rows[1])
    project(far, 2, 6, member_rows[1])
    own_queries(1, 1 - core)
    own_half = pl.multiple_of(core * HALF, HALF)
    pair_q = give(1, r.dqkv.at[:, pl.ds(theirs, HALF)], r.d_q.at[high_rows])
    pair_a = [give(2, r.att.at[:, pl.ds(theirs, HALF)], r.att_o.at[:, pl.ds(theirs, HALF)])]
    own_queries(1, core)
    sth += send_stat(1)
    pair_a.append(give(3, r.att.at[:, pl.ds(own_half, HALF)], r.att_o.at[:, pl.ds(own_half, HALF)]))

    def mine(ref, at, begin):
        return jnp.where(core == 0, ref[at, begin : begin + HALF], ref[at, begin + HALF : begin + 2 * HALF])

    r.d_o[:ROWS] = mine(r.daf_b.at[1], slice(0, ROWS), 0)
    r.d_q[:ROWS] = mine(r.dqkv, slice(0, ROWS), 0)

    def terms(wave, p, dest):
        at = pl.ds(pl.multiple_of(dest * 256, 256), 256)
        if wave == 0:
            if p == 0:
                return [dot(r.xt[0][at, :], r.d_q[:, :384])]
            if p == 1:
                return [dot(r.xt[1][at, :], r.d_q[:, 384:]), dot(r.at[0][at, :], r.d_o[:, :256])]
            return [dot(r.at[1][at, :], r.d_o[:, 256:]), dot(r.ft[at, :], r.cr_rows[...])]
        if p == 0:
            return [dot(r.xt[0][at, :], r.d_k[:, :384])]
        if p == 1:
            return [dot(r.xt[1][at, :], r.d_k[:, 384:]), dot(r.xt[1][at, :], r.d_v[:, :256])]
        return [dot(r.xt[2][at, :], r.d_v[:, 256:])]

    def push(wave, p, slot, src, dst, device):
        slot = (wave * 3 + p) * 16 + slot
        return start(remote(src, dst, r.ring_s.at[slot], r.ring_r.at[slot], device))

    def neighbour(p, phase, offset):
        axis = ORDERS[p][phase]
        return place.partner(axis, place.ahead(axis, offset))

    def put(ref, index, values, dtype, rows=slice(None)):
        begin = 0
        for value in values:
            end = begin + value.shape[1]
            ref[index, rows, begin:end] = value.astype(dtype)
            begin = end

    def go(wave, copies, p, slot, offset):
        copies[p, slot] = push(
            wave, p, slot, r.send1[wave][p].at[slot], r.recv1[wave][p].at[slot], neighbour(p, 0, offset)
        )

    def first_relayed(wave, copies, p):
        values = terms(wave, p, place.ahead(ORDERS[p][0], 2))
        put(r.send1[wave][p], 0, [v[:128] for v in values], BF16)
        put(r.send1[wave][p], 1, [v[128:] for v in values], BF16)
        go(wave, copies, p, 0, 1)
        go(wave, copies, p, 1, 3)

    def first_direct(wave, copies, p):
        values = terms(wave, p, place.ahead(ORDERS[p][0], 1))
        put(r.send1[wave][p], 2, [v[128:] for v in values], BF16)
        put(r.hold[wave][p], 0, [v[:128] for v in values], F32)
        go(wave, copies, p, 2, 1)
        values = terms(wave, p, place.ahead(ORDERS[p][0], 3))
        put(r.send1[wave][p], 3, [v[:128] for v in values], BF16)
        put(r.hold[wave][p], 1, [v[128:] for v in values], F32)
        go(wave, copies, p, 3, 3)

    def relay(wave, copies, parts=(0, 1, 2)):
        for p in parts:
            for half, offset in ((0, 1), (1, 3)):
                copies[p, half].wait_recv()
                r.send1[wave][p][4 + half] = (r.hold[wave][p][half] + r.recv1[wave][p][half].astype(F32)).astype(BF16)
                copies[p, 4 + half] = push(
                    wave, p, 4 + half, r.send1[wave][p].at[4 + half], r.recv1[wave][p].at[4 + half],
                    neighbour(p, 0, offset),
                )

    def own_terms(wave):
        for p in range(3):
            begin = 0
            for value in terms(wave, p, place.at[ORDERS[p][0]]):
                end = begin + value.shape[1]
                r.acc1[wave][p][:, begin:end] = value
                begin = end

    def second(wave, arrivals):
        copies = {}
        for p in range(3):
            acc, came = r.acc1[wave][p], r.recv1[wave][p]
            for slot in (2, 3, 4, 5):
                arrivals[p, slot].wait_recv()
            acc[:128] += came[3].astype(F32) + came[4].astype(F32)
            acc[128:] += came[2].astype(F32) + came[5].astype(F32)
            for offset in (2, 1, 3):
                dest = place.ahead(ORDERS[p][1], offset)
                r.send2[wave][p][offset - 1] = acc[pl.ds(pl.multiple_of(dest * 64, 64), 64), :].astype(BF16)
                copies[p, offset] = push(
                    wave, p, 5 + offset, r.send2[wave][p].at[offset - 1], r.recv2[wave][p].at[offset - 1],
                    neighbour(p, 1, offset),
                )
        return copies

    def third(wave, arrivals):
        copies = []
        for p in range(3):
            for offset in (1, 2, 3):
                arrivals[p, offset].wait_recv()
            own = r.acc1[wave][p][pl.ds(pl.multiple_of(place.at[ORDERS[p][1]] * 64, 64), 64), :]
            came = r.recv2[wave][p]
            r.acc2[wave][p][...] = own + (came[0].astype(F32) + came[1].astype(F32) + came[2].astype(F32))
            for offset in (2, 1, 3, 0):
                dest = place.ahead(ORDERS[p][2], offset)
                device = neighbour(p, 2, offset)
                for other in ((0, 1) if offset else (1,)):
                    side = core if other == 0 else 1 - core
                    slot = 3 + offset if other else offset - 1
                    src = r.acc2[wave][p].at[pl.ds(pl.multiple_of(dest * 16 + side * 8, 8), 8)]
                    to = (device[0], device[1] + (side - core))
                    copies.append(push(wave, p, 9 + slot, src, r.recv3[wave][p].at[slot], to))
        return copies

    def finish(wave, arrivals):
        for copy in arrivals:
            copy.wait_recv()
        own, other = [], []
        for p in range(3):
            came = r.recv3[wave][p]
            at = pl.ds(pl.multiple_of(place.at[ORDERS[p][2]] * 16 + core * 8, 8), 8)
            own.append(r.acc2[wave][p][at, :] + came[0] + came[1] + came[2])
            other.append(came[3] + came[4] + came[5] + came[6])
        return own, other

    def place_both(out, begin, own, other):
        width = own.shape[1]
        out[:, begin : begin + width] = jnp.where(core == 0, own, other)
        out[:, begin + HALF : begin + HALF + width] = jnp.where(core == 0, other, own)

    arrive0 = {}
    pair_q.wait_recv()
    first_relayed(0, arrive0, 0)
    first_direct(0, arrive0, 0)
    lay(r.att[...], ats, 0)
    pair_o.wait_recv()
    for copy in pair_a:
        copy.wait_recv()
    lay(r.att_o[...], ats, ROWS)
    first_relayed(0, arrive0, 1)
    after = r.lat[1].astype(F32) + dot(r.att[...], r.w_back[...])
    lay(after.astype(BF16), [(r.ft, ORDERS[2])], 0)
    first_relayed(0, arrive0, 2)
    first_direct(0, arrive0, 1)
    first_direct(0, arrive0, 2)

    for side, copy in ((near, crh_near), (far, crh_far)):
        copy.wait_recv()
        decode(side)
        attend_back(side)
    project(far, 0, 2)

    def other_queries(half, members=(0, 1)):
        for m in members:
            rows = member_rows[m]
            for u in range(2):
                cols = group_cols(half, u)
                keys = r.kx[1, rows, cols]
                values = r.vx[1, rows, cols]
                dk = r.dk_acc[rows, cols]
                dv = r.dv_acc[rows, cols]
                for side in range(2):
                    q_b = spread(r.qx[2 * side, rows, cols])
                    d_b = spread(r.dx[2 * side, rows, cols])
                    lse = r.stat_n[side, m, half, 2 * u : 2 * u + 1, :]
                    delta = r.stat_n[side, m, half, 2 * u + 1 : 2 * u + 2, :]
                    prob = jnp.exp2(dot_nt(keys, q_b) * LOG2E - (lse - edge[side]))
                    dscore = (prob * (dot_nt(values, d_b) - delta)).astype(BF16)
                    dk += dot(dscore, q_b)
                    dv += dot(prob.astype(BF16), d_b)
                r.dqkv[rows, group_cols(half, u, WIDTH)] = dk.astype(BF16)
                r.dqkv[rows, group_cols(half, u, 2 * WIDTH)] = dv.astype(BF16)

    for copy in sth:
        copy.wait_recv()
    relay(0, arrive0, (0,))
    other_queries(1 - core, (0,))
    relay(0, arrive0, (1,))
    other_queries(1 - core, (1,))
    pair_k = give(4, r.dqkv.at[:, pl.ds(pl.multiple_of(WIDTH + theirs, HALF), HALF)], r.d_k.at[high_rows])
    pair_v = give(5, r.dqkv.at[:, pl.ds(pl.multiple_of(2 * WIDTH + theirs, HALF), HALF)], r.d_v.at[high_rows])
    relay(0, arrive0, (2,))
    other_queries(core)
    r.d_k[:ROWS] = mine(r.dqkv, slice(0, ROWS), WIDTH)
    r.d_v[:ROWS] = mine(r.dqkv, slice(0, ROWS), 2 * WIDTH)
    pair_k.wait_recv()
    pair_v.wait_recv()
    arrive1 = {}
    for p in range(3):
        first_relayed(1, arrive1, p)
    for p in range(3):
        first_direct(1, arrive1, p)
    own_terms(0)
    arrive0 = second(0, arrive0)
    own_terms(1)

    for j in range(4):
        at = slice(j * GROUP, (j + 1) * GROUP)
        r.dnorm[:, at] = dot_nt(r.dqkv[...], r.w_in[at, :])
    relay(1, arrive1)
    arrive0 = third(0, arrive0)
    dnorm = r.dnorm[...]
    norm = r.norm[...]
    dlayer = r.rstd[:, :1] * (
        dnorm
        - jnp.mean(dnorm, axis=-1, keepdims=True)
        - norm * jnp.mean(dnorm * norm, axis=-1, keepdims=True)
    )
    r.g_stage[...] = (r.daf[...] + dlayer).astype(BF16)
    stored = pltpu.make_async_copy(r.g_stage, g_latent, load.at[8])
    stored.start()

    arrive1 = second(1, arrive1)
    own, other = finish(0, arrive0)
    place_both(g_qkv, 0, own[0], other[0])
    place_both(g_qkv, 384, own[1][:, :128], other[1][:, :128])
    place_both(g_o, 0, own[1][:, 128:], other[1][:, 128:])
    place_both(g_o, 256, own[2][:, :256], other[2][:, :256])
    total = own[2][:, 256:] + other[2][:, 256:]
    g_out[...] = total[:, :channels]

    arrive1 = third(1, arrive1)
    own, other = finish(1, arrive1)
    place_both(g_qkv, WIDTH, own[0], other[0])
    place_both(g_qkv, WIDTH + 384, own[1][:, :128], other[1][:, :128])
    place_both(g_qkv, 2 * WIDTH, own[1][:, 128:], other[1][:, 128:])
    place_both(g_qkv, 2 * WIDTH + 256, own[2], other[2])
    stored.wait()
    for copy in sent:
        copy.wait_send()


def hand_over(*refs):
    for source, target in zip(refs[:4], refs[4:]):
        target[...] = source[...]


def on_device(latent, predictions, target, area_weight, slab_count, w_qkv, w_o, w_out):
    members_here, points, width = latent.shape
    channels = predictions.shape[1]
    rows = members_here * points
    vmem = pl.BlockSpec(memory_space=pltpu.VMEM)
    hbm = pl.BlockSpec(memory_space=pl.ANY)
    smem = pl.BlockSpec(memory_space=pltpu.SMEM)
    shapes = (
        jax.ShapeDtypeStruct((rows, width), BF16),
        jax.ShapeDtypeStruct((8, 3 * width), F32),
        jax.ShapeDtypeStruct((8, width), F32),
        jax.ShapeDtypeStruct((8, channels), F32),
    )
    grad_latent, grad_qkv, grad_o, grad_out = pl.pallas_call(
        kernel,
        out_shape=shapes,
        in_specs=[hbm, hbm, hbm, vmem, smem, hbm, hbm, hbm],
        out_specs=[hbm, vmem, vmem, vmem],
        scratch_shapes=SHAPES,
        compiler_params=pltpu.CompilerParams(
            collective_id=0, has_side_effects=True, vmem_limit_bytes=62 * 1024 * 1024
        ),
    )(
        latent.reshape(rows, width), predictions.transpose(1, 0, 2).reshape(members_here * channels, points), target, area_weight.reshape(1, points),
        slab_count, w_qkv, w_o, w_out.T,
    )
    grad_latent, grad_qkv, grad_o, grad_out = pl.pallas_call(
        hand_over,
        out_shape=shapes,
        in_specs=[vmem] * 4,
        out_specs=[vmem] * 4,
    )(grad_latent, grad_qkv, grad_o, grad_out)
    return grad_latent.reshape(latent.shape), grad_qkv, grad_o, grad_out


def solution(mesh):
    placed = (
        P("member", "space", None),
        P("member", None, "space"),
        P(None, "space"),
        P("space"),
        P("space"),
        P(),
        P(),
        P(),
    )
    return jax.shard_map(
        on_device,
        mesh=mesh,
        in_specs=placed,
        out_specs=(
            P("member", "space", None),
            P(("member", "space"), None),
            P(("member", "space"), None),
            P(("member", "space"), None),
        ),
        check_vma=False,
    )
```
